1024 devices in a mesh: modes: 128 (over z, y, core), grid: 8 (over x).
Axes of the slice: x: 8, y: 8, z: 8, core: 2. Of those that a mesh axis runs over, the one named last changes fastest.
Arguments:
- u_modes: float32 [128, 2, 64, 1024], P('modes', None, 'grid'), may hold values from -5 to 5
- v_modes: float32 [128, 2, 64, 1024], P('modes', None, 'grid'), may hold values from -0.85 to 0.85
- potential: float32 [64, 1024], P('grid'), may hold values from -1.5 to 0
- pairing: float32 [2, 64, 1024], P(None, 'grid'), may hold values from -1 to 1
Outputs:
- u_next: float32 [128, 2, 64, 1024], P('modes', None, 'grid')
- v_next: float32 [128, 2, 64, 1024], P('modes', None, 'grid')
- fields: float32 [4, 64, 1024], P(None, 'grid')
The draws below stay inside these ranges and needn't reach their ends.
All inputs are finite; a program needn't handle non-finite values.
Results may differ from the reference program's by a relative error of at most 0.00035.
Values sent between devices are 32-bit elements; how exact they have to be, the bound alone decides.
A program may use at most 64 MiB of HBM per device.

```python
import jax
import jax.numpy as jnp
from jax import lax

MODE_DEV = 1
NX = 32
NY = 32
NZ = 64
NXY = 1024
MODES = 128
N_MODES = 128


def mode_pair(key):
    base_key = jax.random.fold_in(key, 11)
    first_key, mixing_key, jitter_key = jax.random.split(base_key, 3)
    full_shape = (MODES, 2, NZ, NX * NY)
    upper = jax.random.truncated_normal(first_key, -5.0, 5.0, full_shape, jnp.float32)
    mixing = jax.random.uniform(mixing_key, full_shape, jnp.float32, 0.02, 0.06)
    jitter = 0.1 * jax.random.truncated_normal(jitter_key, -5.0, 5.0, full_shape, jnp.float32)
    return (upper, mixing * upper + jitter)


def draw_u_modes(key, part):
    return mode_pair(key)[0]


def draw_v_modes(key, part):
    return mode_pair(key)[1]


def level_of(key, extent, pieces, smallest, largest):
    factor_of, own = 1.0, jax.random.fold_in(key, 6)
    for dim, blocks in pieces:
        steps = jnp.exp(jax.random.uniform(jax.random.fold_in(own, dim), (blocks,), jnp.float32, smallest / len(pieces), largest / len(pieces)))
        factor_of = factor_of * jnp.repeat(steps, extent[dim] // blocks).reshape([-1 if axis == dim else 1 for axis in range(len(extent))])
    return factor_of


def setup_inputs(seed: int = 0) -> dict:
    keys = jax.random.split(jax.random.key(seed), 5)
    return {
        "u_modes": draw_u_modes(jax.random.fold_in(keys[4], 71), 0),
        "v_modes": draw_v_modes(jax.random.fold_in(keys[4], 71), 0),
        "potential": jnp.clip(-1.5 + 1.5 * jax.random.uniform(keys[2], (NZ, NXY), jnp.float32) ** level_of(keys[2], (NZ, NXY), ((0, 8),), -0.2, 0.2), -1.5, 0.0),
        "pairing": jnp.clip(jax.random.uniform(keys[3], (2, NZ, NXY), jnp.float32, -1.0, 1.0) * level_of(keys[3], (2, NZ, NXY), ((1, 8),), -0.4, 0.0), -1.0, 1.0),
    }


stencil_coef = (-205.0 / 72.0, 8.0 / 5.0, -1.0 / 5.0, 8.0 / 315.0, -1.0 / 560.0)
alpha_coef = 1.14
beta_coef = -0.553
gamma_coef = -11.11
time_step = 0.18
epsilon = 1e-6


def laplace_ref(states):
    shaped = states.reshape(states.shape[:3] + (NY, NX))
    total = 3.0 * stencil_coef[0] * shaped
    for offset in range(1, 5):
        for axis_num in (2, 3, 4):
            total = total + stencil_coef[offset] * (jnp.roll(shaped, offset, axis_num) + jnp.roll(shaped, -offset, axis_num))
    return total.reshape(states.shape)


def slopes(states, laplace, field_pot, pair_re, pair_im):
    kinetic = -0.5 * alpha_coef * laplace + field_pot * states
    upper_re = kinetic[:, 0] + pair_re * states[:, 2] - pair_im * states[:, 3]
    upper_im = kinetic[:, 1] + pair_re * states[:, 3] + pair_im * states[:, 2]
    lower_re = pair_re * states[:, 0] + pair_im * states[:, 1] - kinetic[:, 2]
    lower_im = pair_re * states[:, 1] - pair_im * states[:, 0] - kinetic[:, 3]
    return jnp.stack([upper_im, -upper_re, lower_im, -lower_re], axis=1)


def potentials(raw_sums, modes_total):
    density = 2.0 * raw_sums[0] / modes_total
    kinetic = -2.0 * raw_sums[1] / modes_total
    anomal_re = raw_sums[2] / modes_total
    anomal_im = raw_sums[3] / modes_total
    dense_safe = density + epsilon
    fermi = 0.5 * jnp.power(3.0 * jnp.pi ** 2 * dense_safe, 2.0 / 3.0)
    anomal_sq = anomal_re * anomal_re + anomal_im * anomal_im
    third_root = jnp.power(dense_safe, -1.0 / 3.0)
    field_pot = beta_coef * fermi - (gamma_coef / 3.0) * anomal_sq * third_root / dense_safe
    pair_re = -gamma_coef * anomal_re * third_root
    pair_im = -gamma_coef * anomal_im * third_root
    energy = alpha_coef * kinetic / 2.0 + 0.6 * beta_coef * dense_safe * fermi + gamma_coef * anomal_sq * third_root
    return jnp.stack([field_pot, pair_re, pair_im, energy], axis=0)


def reference(u_modes, v_modes, potential, pairing):
    u_blocks = u_modes.reshape((N_MODES, MODE_DEV) + u_modes.shape[1:])
    v_blocks = v_modes.reshape((N_MODES, MODE_DEV) + v_modes.shape[1:])

    def evolve(pair_in):
        start_state = jnp.concatenate([pair_in[0], pair_in[1]], axis=1)

        def slope_at(states):
            return slopes(states, laplace_ref(states), potential, pairing[0], pairing[1])

        slope_one = slope_at(start_state)
        slope_two = slope_at(start_state + 0.5 * time_step * slope_one)
        slope_three = slope_at(start_state + 0.5 * time_step * slope_two)
        slope_four = slope_at(start_state + time_step * slope_three)
        return start_state + (time_step / 6.0) * (slope_one + 2.0 * slope_two + 2.0 * slope_three + slope_four)

    stepped_all = lax.map(evolve, (u_blocks, v_blocks))

    def add_sums(running, stepped):
        lap_step = laplace_ref(stepped)
        partial_value = jnp.stack([
            jnp.sum(stepped[:, 2] * stepped[:, 2] + stepped[:, 3] * stepped[:, 3], axis=0),
            jnp.sum(stepped[:, 2] * lap_step[:, 2] + stepped[:, 3] * lap_step[:, 3], axis=0),
            jnp.sum(stepped[:, 0] * stepped[:, 2] + stepped[:, 1] * stepped[:, 3], axis=0),
            jnp.sum(stepped[:, 1] * stepped[:, 2] - stepped[:, 0] * stepped[:, 3], axis=0),
        ], axis=0)
        return running + partial_value, None

    zero_sums = jnp.zeros((4,) + potential.shape, jnp.float32)
    raw_sums, unused = lax.scan(add_sums, zero_sums, stepped_all)
    fields = potentials(raw_sums, float(MODES))

    def advance(stepped):
        lap_step = laplace_ref(stepped)
        next_one = slopes(stepped, lap_step, fields[0], fields[1], fields[2])
        middle = stepped + 0.5 * time_step * next_one
        next_two = slopes(middle, laplace_ref(middle), fields[0], fields[1], fields[2])
        return stepped + (time_step / 6.0) * (next_one + 2.0 * next_two)

    result = lax.map(advance, stepped_all)
    result = result.reshape((MODES,) + result.shape[2:])
    return result[:, 0:2], result[:, 2:4], fields
```

```python
import functools
import math

import jax
import jax.numpy as jnp
from jax import lax
from jax.experimental import pallas as pl
from jax.experimental.pallas import tpu as pltpu
from jax.sharding import PartitionSpec as P

MESH = pl.DeviceIdType.MESH
COEF = (-205.0 / 72.0, 8.0 / 5.0, -1.0 / 5.0, 8.0 / 315.0, -1.0 / 560.0)
ALPHA = 1.14
BETA = -0.553
GAMMA = -11.11
DT = 0.18
EPS = 1e-06
PLANES = 8
ROWS = 8
LANES = 128


def in_plane(x, masks):
    lane32, lane, _ = masks
    total = (3.0 * COEF[0]) * x

    def turn(shift):
        return pltpu.roll(x, shift, 2)

    for k in range(1, 5):
        minus = jnp.where(lane32 >= k, turn(k), turn(96 + k))
        plus = jnp.where(lane32 < 32 - k, turn(128 - k), turn(32 - k))
        total = total + COEF[k] * (minus + plus)
    zero = jnp.float32(0.0)
    up = COEF[4] * x
    down = up
    for j in range(1, 4):
        moved = turn(128 - 32 * j)
        near, far = COEF[j], COEF[4 - j]
        within = lane < 128 - 32 * j
        total = total + jnp.where(within, near, far) * moved
        up = up + jnp.where(within, zero, near) * moved
        down = down + jnp.where(within, far, zero) * moved
    return total + pltpu.roll(up, ROWS - 1, 1) + pltpu.roll(down, 1, 1)


def slope(x, lap, pot, pr, pi):
    kin = [(-0.5 * ALPHA) * lap[c] + pot * x[c] for c in range(4)]
    return [
        kin[1] + pr * x[3] + pi * x[2],
        pi * x[3] - pr * x[2] - kin[0],
        pr * x[1] - pi * x[0] - kin[3],
        kin[2] - pr * x[0] - pi * x[1],
    ]


def kernel(
    n,
    grid_n,
    modes_total,
    u_ref,
    v_ref,
    pot_ref,
    pair_ref,
    uo_ref,
    vo_ref,
    fo_ref,
    raw,
    rows,
    xs,
    pots,
    acc,
    base,
    lap1,
    q1,
    halo_lo,
    halo_hi,
    sums,
    pair_in,
    piece_in,
    gather_in,
    field_mine,
    field_other,
    load_sem,
    halo_send,
    halo_recv,
    pair_sem,
    first_send,
    first_recv,
    second_send,
    second_recv,
    back_send,
    back_recv,
):
    m = lax.axis_index("modes")
    g = lax.axis_index("grid")
    core = lax.rem(m, 2)
    yy = lax.rem(m // 2, n)
    zz = m // (2 * n)
    left = (m, lax.rem(g + grid_n - 1, grid_n))
    right = (m, lax.rem(g + 1, grid_n))
    sibling = (m + 1 - 2 * core, g)
    first = yy + core * (zz - yy)
    second = zz + core * (yy - zz)
    first_base = (1 - core) * zz * 2 * n + core * (yy * 2 + 1)
    first_step = 2 + core * (2 * n - 2)
    second_base = (1 - core) * yy * 2 + core * (zz * 2 * n + 1)
    second_step = 2 * n - core * (2 * n - 2)
    share = PLANES // n

    def first_peer(d):
        return (first_base + lax.rem(first + d, n) * first_step, g)

    def second_peer(d):
        return (second_base + lax.rem(second + d, n) * second_step, g)

    loads = [
        pltpu.make_async_copy(u_ref.at[0], raw.at[0:2], load_sem.at[0]),
        pltpu.make_async_copy(v_ref.at[0], raw.at[2:4], load_sem.at[1]),
        pltpu.make_async_copy(pot_ref, raw.at[4], load_sem.at[2]),
        pltpu.make_async_copy(pair_ref, raw.at[5:7], load_sem.at[3]),
    ]
    for load in loads:
        load.start()

    barrier = pltpu.get_barrier_semaphore()
    partners = [left, right, sibling]
    partners += [first_peer(d) for d in range(1, n)] + [second_peer(d) for d in range(1, n)]
    for partner in partners:
        pl.semaphore_signal(barrier, inc=1, device_id=partner, device_id_type=MESH)

    lane = lax.broadcasted_iota(jnp.int32, (1, ROWS, LANES), 2)
    row = lax.broadcasted_iota(jnp.int32, (ROWS, LANES), 0)
    masks = (lax.rem(lane, 32), lane, None)
    top = row < 4

    for load in loads:
        load.wait()
    for c in range(7):
        for t in range(ROWS):
            rows[c, t * PLANES : (t + 1) * PLANES, :] = raw[c, :, t * LANES : (t + 1) * LANES]
    for c in range(7):
        for z in range(PLANES):
            plane = rows[c, pl.ds(z, ROWS, stride=PLANES), :]
            if c < 4:
                xs[0, z, c] = plane
                acc[z, c] = plane
            else:
                pots[z, c - 4] = plane
    pl.semaphore_wait(barrier, len(partners))

    def to_left(s):
        return pltpu.make_async_remote_copy(
            src_ref=xs.at[s, 0:4],
            dst_ref=halo_hi.at[s],
            send_sem=halo_send.at[0, s],
            recv_sem=halo_recv.at[1, s],
            device_id=left,
            device_id_type=MESH,
        )

    def to_right(s):
        return pltpu.make_async_remote_copy(
            src_ref=xs.at[s, 4:8],
            dst_ref=halo_lo.at[s],
            send_sem=halo_send.at[1, s],
            recv_sem=halo_recv.at[0, s],
            device_id=right,
            device_id_type=MESH,
        )

    def own_part(s):
        def plane_part(z, carry):
            base[z] = in_plane(xs[s, z], masks)
            return carry

        lax.fori_loop(0, PLANES, plane_part, 0)
        for z in range(PLANES):
            total = base[z]
            for k in range(1, 5):
                if z - k >= 0 and z + k < PLANES:
                    total = total + COEF[k] * (xs[s, z - k] + xs[s, z + k])
                elif z - k >= 0:
                    total = total + COEF[k] * xs[s, z - k]
                elif z + k < PLANES:
                    total = total + COEF[k] * xs[s, z + k]
            base[z] = total

    def with_halo(s, z):
        total = base[z]
        for k in range(1, 5):
            if z - k < 0:
                total = total + COEF[k] * halo_lo[s, 4 + z - k]
            if z + k >= PLANES:
                total = total + COEF[k] * halo_hi[s, z + k - PLANES]
        return total

    to_left(0).start()
    to_right(0).start()

    def stage(s, carry):
        own_part(s)
        last = s == 3
        reach = jnp.where(s == 2, DT, 0.5 * DT).astype(jnp.float32)
        weight = jnp.where((s == 0) | last, DT / 6.0, DT / 3.0).astype(jnp.float32)
        for side in (0, 1):
            (to_right if side == 0 else to_left)(s).wait_recv()
            for z in range(4 * side, 4 * side + 4):
                x = xs[s, z]
                k = slope(x, with_halo(s, z), pots[z, 0], pots[z, 1], pots[z, 2])
                for c in range(4):
                    total = acc[z, c] + weight * k[c]
                    acc[z, c] = total
                    xs[s + 1, z, c] = jnp.where(last, total, xs[0, z, c] + reach * k[c])
            (to_left if side == 0 else to_right)(s + 1).start()
        return carry

    lax.fori_loop(0, 4, stage, 0)

    own_part(4)
    for side in (0, 1):
        (to_right if side == 0 else to_left)(4).wait_recv()
        for z in range(4 * side, 4 * side + 4):
            x = xs[4, z]
            lap = with_halo(4, z)
            lap1[z] = lap
            four = [
                x[2] * x[2] + x[3] * x[3],
                x[2] * lap[2] + x[3] * lap[3],
                x[0] * x[2] + x[1] * x[3],
                x[1] * x[2] - x[0] * x[3],
            ]
            for p in range(2):
                a, b = four[2 * p], four[2 * p + 1]
                sums[0, z, p] = jnp.where(top, a, pltpu.roll(b, 4, 0))
                sums[1, z, p] = jnp.where(top, pltpu.roll(a, 4, 0), b)
    pair_copy = pltpu.make_async_remote_copy(
        src_ref=sums.at[1 - core],
        dst_ref=pair_in,
        send_sem=pair_sem.at[0],
        recv_sem=pair_sem.at[1],
        device_id=sibling,
        device_id_type=MESH,
    )
    pair_copy.start()
    pair_copy.wait_recv()
    pair_in[...] = pair_in[...] + sums[core]

    order = sorted(range(1, n), key=lambda d: -min(d, n - d))
    first_copies = []
    for d in order:
        copy = pltpu.make_async_remote_copy(
            src_ref=pair_in.at[pl.ds(lax.rem(first + d, n) * share, share)],
            dst_ref=piece_in.at[d - 1],
            send_sem=first_send.at[d - 1],
            recv_sem=first_recv.at[d - 1],
            device_id=first_peer(d),
            device_id_type=MESH,
        )
        copy.start()
        first_copies.append(copy)
    total = pair_in[pl.ds(first * share, share)]
    for copy in reversed(first_copies):
        copy.wait_recv()
    for d in range(1, n):
        total = total + piece_in[d - 1]
    gather_in[0] = total

    second_copies = []
    for d in order:
        copy = pltpu.make_async_remote_copy(
            src_ref=gather_in.at[0],
            dst_ref=gather_in.at[d],
            send_sem=second_send.at[d - 1],
            recv_sem=second_recv.at[d - 1],
            device_id=second_peer(d),
            device_id_type=MESH,
        )
        copy.start()
        second_copies.append(copy)
    for copy in reversed(second_copies):
        copy.wait_recv()
    total = gather_in[second]
    for i in range(1, n):
        total = total + gather_in[lax.rem(second + n - i, n)]

    for z in range(share):
        s01, s23 = total[z, 0], total[z, 1]
        density = (2.0 / modes_total) * s01
        kinetic = (-2.0 / modes_total) * pltpu.roll(s01, 4, 0)
        an_re = (1.0 / modes_total) * s23
        an_im = (1.0 / modes_total) * pltpu.roll(s23, 4, 0)
        dense = jnp.where(top, density, jnp.float32(1.0)) + EPS
        third_root = jnp.exp(jnp.log(dense) * (-1.0 / 3.0))
        fermi = (0.5 * (3.0 * math.pi**2) ** (2.0 / 3.0)) * (dense * third_root)
        an_sq = an_re * an_re + an_im * an_im
        f0 = BETA * fermi - (GAMMA / 3.0) * an_sq * third_root / dense
        f1 = -GAMMA * an_re * third_root
        f2 = -GAMMA * an_im * third_root
        f3 = (0.5 * ALPHA) * kinetic + (0.6 * BETA) * dense * fermi + GAMMA * an_sq * third_root
        field_mine[0, z, 0] = jnp.where(top, f0, pltpu.roll(f1, 4, 0))
        field_mine[0, z, 1] = jnp.where(top, f2, pltpu.roll(f3, 4, 0))

    back_copies = []
    for d in order:
        copy = pltpu.make_async_remote_copy(
            src_ref=field_mine.at[0],
            dst_ref=field_mine.at[d],
            send_sem=back_send.at[d - 1],
            recv_sem=back_recv.at[d - 1],
            device_id=first_peer(d),
            device_id_type=MESH,
        )
        copy.start()
        back_copies.append(copy)
    for copy in reversed(back_copies):
        copy.wait_recv()
    pair_back = pltpu.make_async_remote_copy(
        src_ref=field_mine,
        dst_ref=field_other,
        send_sem=pair_sem.at[2],
        recv_sem=pair_sem.at[3],
        device_id=sibling,
        device_id_type=MESH,
    )
    pair_back.start()
    pair_back.wait_recv()

    even = core == 0
    for z in range(PLANES):
        place, part = z // share, z % share
        mine = field_mine[lax.rem(first + n - place, n), part]
        other = field_other[lax.rem(second + n - place, n), part]
        fields = []
        for p in range(2):
            low = jnp.where(even, mine[p], other[p])
            high = jnp.where(even, other[p], mine[p])
            fields.append(jnp.where(top, low, pltpu.roll(high, 4, 0)))
            fields.append(jnp.where(top, pltpu.roll(low, 4, 0), high))
        for c in range(3):
            pots[z, c] = fields[c]
        for c in range(4):
            rows[c, z * ROWS : (z + 1) * ROWS, :] = fields[c]
        x = xs[4, z]
        k = slope(x, lap1[z], fields[0], fields[1], fields[2])
        for c in range(4):
            q1[z, c] = k[c]
            xs[5, z, c] = x[c] + (0.5 * DT) * k[c]
        if z == 3:
            to_left(5).start()
    to_right(5).start()
    for c in range(4):
        for t in range(ROWS):
            fo_ref[c, :, t * LANES : (t + 1) * LANES] = rows[c, pl.ds(t, PLANES, stride=ROWS), :]
    own_part(5)
    for side in (0, 1):
        (to_right if side == 0 else to_left)(5).wait_recv()
        for z in range(4 * side, 4 * side + 4):
            k = slope(xs[5, z], with_halo(5, z), pots[z, 0], pots[z, 1], pots[z, 2])
            for c in range(4):
                out = xs[4, z, c] + (DT / 6.0) * (q1[z, c] + 2.0 * k[c])
                rows[c, z * ROWS : (z + 1) * ROWS, :] = out
    for c in range(4):
        for t in range(ROWS):
            block = rows[c, pl.ds(t, PLANES, stride=ROWS), :]
            if c < 2:
                uo_ref[0, c, :, t * LANES : (t + 1) * LANES] = block
            else:
                vo_ref[0, c - 2, :, t * LANES : (t + 1) * LANES] = block

    for s in range(6):
        to_left(s).wait_send()
        to_right(s).wait_send()
    pair_copy.wait_send()
    pair_back.wait_send()
    for copy in first_copies + second_copies + back_copies:
        copy.wait_send()


def solution(mesh):
    modes, grid_n = mesh.shape["modes"], mesh.shape["grid"]
    n = math.isqrt(modes // 2)
    share = PLANES // n
    f32 = jnp.float32
    plane = (ROWS, LANES)

    def local(u_modes, v_modes, potential, pairing):
        vmem = pl.BlockSpec(memory_space=pltpu.VMEM)
        return pl.pallas_call(
            functools.partial(kernel, n, grid_n, float(modes)),
            out_shape=(
                jax.ShapeDtypeStruct(u_modes.shape, f32),
                jax.ShapeDtypeStruct(v_modes.shape, f32),
                jax.ShapeDtypeStruct((4,) + potential.shape, f32),
            ),
            in_specs=[pl.BlockSpec(memory_space=pl.ANY)] * 4,
            out_specs=(vmem, vmem, vmem),
            scratch_shapes=[
                pltpu.VMEM((7, PLANES, ROWS * LANES), f32),
                pltpu.VMEM((7, PLANES * ROWS, LANES), f32),
                pltpu.VMEM((6, PLANES, 4) + plane, f32),
                pltpu.VMEM((PLANES, 3) + plane, f32),
                pltpu.VMEM((PLANES, 4) + plane, f32),
                pltpu.VMEM((PLANES, 4) + plane, f32),
                pltpu.VMEM((PLANES, 4) + plane, f32),
                pltpu.VMEM((PLANES, 4) + plane, f32),
                pltpu.VMEM((6, 4, 4) + plane, f32),
                pltpu.VMEM((6, 4, 4) + plane, f32),
                pltpu.VMEM((2, PLANES, 2) + plane, f32),
                pltpu.VMEM((PLANES, 2) + plane, f32),
                pltpu.VMEM((n - 1, share, 2) + plane, f32),
                pltpu.VMEM((n, share, 2) + plane, f32),
                pltpu.VMEM((n, share, 2) + plane, f32),
                pltpu.VMEM((n, share, 2) + plane, f32),
                pltpu.SemaphoreType.DMA((4,)),
                pltpu.SemaphoreType.DMA((2, 6)),
                pltpu.SemaphoreType.DMA((2, 6)),
                pltpu.SemaphoreType.DMA((4,)),
                pltpu.SemaphoreType.DMA((n - 1,)),
                pltpu.SemaphoreType.DMA((n - 1,)),
                pltpu.SemaphoreType.DMA((n - 1,)),
                pltpu.SemaphoreType.DMA((n - 1,)),
                pltpu.SemaphoreType.DMA((n - 1,)),
                pltpu.SemaphoreType.DMA((n - 1,)),
            ],
            compiler_params=pltpu.CompilerParams(
                collective_id=0, has_side_effects=True, vmem_limit_bytes=32 * 1024 * 1024
            ),
        )(u_modes, v_modes, potential, pairing)

    placed = (
        P("modes", None, "grid", None),
        P("modes", None, "grid", None),
        P("grid", None),
        P(None, "grid", None),
    )
    return jax.shard_map(
        local,
        mesh=mesh,
        in_specs=placed,
        out_specs=(placed[0], placed[1], placed[3]),
        check_vma=False,
    )
```

```python
import functools
import math

import jax
import jax.numpy as jnp
from jax import lax
from jax.experimental import pallas as pl
from jax.experimental.pallas import tpu as pltpu
from jax.sharding import PartitionSpec as P

MESH = pl.DeviceIdType.MESH
COEF = (-205.0 / 72.0, 8.0 / 5.0, -1.0 / 5.0, 8.0 / 315.0, -1.0 / 560.0)
ALPHA = 1.14
BETA = -0.553
GAMMA = -11.11
DT = 0.18
EPS = 1e-06
PLANES = 8
ROWS = 8
LANES = 128


def spread(weights):
    source = lax.broadcasted_iota(jnp.int32, (LANES, LANES), 0)
    target = lax.broadcasted_iota(jnp.int32, (LANES, LANES), 1)
    dx = lax.rem(lax.rem(source, 32) + 32 - lax.rem(target, 32), 32)
    dy = source // 32 - target // 32
    zero = jnp.zeros((LANES, LANES), jnp.float32)
    within, above, below = zero, zero, zero
    for k in range(1, 5):
        within = jnp.where((dy == 0) & ((dx == k) | (dx == 32 - k)), COEF[k], within)
        within = jnp.where((dx == 0) & ((dy == k) | (dy == -k)), COEF[k], within)
        above = jnp.where((dx == 0) & (dy + 4 == k), COEF[k], above)
        below = jnp.where((dx == 0) & (4 - dy == k), COEF[k], below)
    for i, part in enumerate((within, above, below)):
        high = part.astype(jnp.bfloat16)
        low = (part - high.astype(jnp.float32)).astype(jnp.bfloat16)
        for half in range(2):
            weights[i, LANES * half : LANES * (half + 1), 0:LANES] = high
            weights[i, LANES * half : LANES * (half + 1), LANES : 2 * LANES] = low


def in_plane(x, weights):
    flat = x.reshape(-1, LANES)
    high = flat.astype(jnp.bfloat16)
    low = (flat - high.astype(jnp.float32)).astype(jnp.bfloat16)
    both = jnp.concatenate([high, low], axis=1)

    def times(i):
        wide = jnp.dot(both, weights[i], preferred_element_type=jnp.float32)
        return (wide[:, :LANES] + wide[:, LANES:]).reshape(x.shape)

    return (3.0 * COEF[0]) * x + times(0) + pltpu.roll(times(1), ROWS - 1, 1) + pltpu.roll(times(2), 1, 1)


def slope(x, lap, pot, pr, pi):
    kin = [(-0.5 * ALPHA) * lap[c] + pot * x[c] for c in range(4)]
    return [
        kin[1] + pr * x[3] + pi * x[2],
        pi * x[3] - pr * x[2] - kin[0],
        pr * x[1] - pi * x[0] - kin[3],
        kin[2] - pr * x[0] - pi * x[1],
    ]


def turned(h):
    return [h[1], -h[0], -h[3], h[2]]


def kernel(
    n,
    grid_n,
    modes_total,
    u_ref,
    v_ref,
    pot_ref,
    pair_ref,
    out_rows,
    field_rows,
    raw,
    rows,
    xs,
    pots,
    acc,
    base,
    pre,
    halo_lo,
    halo_hi,
    sums,
    piece_in,
    gather_in,
    field_mine,
    field_other,
    weights,
    load_sem,
    halo_send,
    halo_recv,
    first_send,
    first_recv,
    second_send,
    second_recv,
    back_send,
    back_recv,
):
    m = lax.axis_index("modes")
    g = lax.axis_index("grid")
    core = lax.rem(m, 2)
    yy = lax.rem(m // 2, n)
    zz = m // (2 * n)
    left = (m, lax.rem(g + grid_n - 1, grid_n))
    right = (m, lax.rem(g + 1, grid_n))
    flip = 1 - 2 * core
    first = yy + core * (zz - yy)
    second = zz + core * (yy - zz)
    first_base = (1 - core) * zz * 2 * n + core * (yy * 2 + 1)
    first_step = 2 + core * (2 * n - 2)
    second_base = (1 - core) * yy * 2 + core * (zz * 2 * n + 1)
    second_step = 2 * n - core * (2 * n - 2)
    share = PLANES // n
    first_at = [lax.rem(first + d, n) for d in range(n)]
    second_at = [lax.rem(second + d, n) for d in range(n)]
    first_peer = [(first_base + at * first_step, g) for at in first_at]
    second_peer = [(second_base + at * second_step, g) for at in second_at]
    first_cross = [(peer[0] + flip, g) for peer in first_peer]
    second_cross = [(peer[0] + flip, g) for peer in second_peer]

    barrier = pltpu.get_barrier_semaphore()
    partners = [left, right] + first_cross + first_peer[1:] + second_peer[1:] + second_cross[1:]
    for partner in partners:
        pl.semaphore_signal(barrier, inc=1, device_id=partner, device_id_type=MESH)

    loads = [
        pltpu.make_async_copy(u_ref.at[0], raw.at[0:2], load_sem.at[0]),
        pltpu.make_async_copy(v_ref.at[0], raw.at[2:4], load_sem.at[1]),
        pltpu.make_async_copy(pot_ref, raw.at[4], load_sem.at[2]),
        pltpu.make_async_copy(pair_ref, raw.at[5:7], load_sem.at[3]),
    ]
    for load in loads:
        load.start()
    spread(weights)

    row = lax.broadcasted_iota(jnp.int32, (ROWS, LANES), 0)
    top = row < 4

    for load in loads:
        load.wait()
    for c in range(7):
        for t in range(ROWS):
            rows[c, t * PLANES : (t + 1) * PLANES, :] = raw[c, :, t * LANES : (t + 1) * LANES]
    for c in range(7):
        for z in range(PLANES):
            plane = rows[c, pl.ds(z, ROWS, stride=PLANES), :]
            if c < 4:
                xs[0, z, c] = plane
                acc[z, c] = plane
            else:
                pots[z, c - 4] = plane
    pl.semaphore_wait(barrier, len(partners))

    def to_left(s):
        return pltpu.make_async_remote_copy(
            src_ref=xs.at[s, 0:4],
            dst_ref=halo_hi.at[s],
            send_sem=halo_send.at[0, s],
            recv_sem=halo_recv.at[1, s],
            device_id=left,
            device_id_type=MESH,
        )

    def to_right(s):
        return pltpu.make_async_remote_copy(
            src_ref=xs.at[s, 4:8],
            dst_ref=halo_lo.at[s],
            send_sem=halo_send.at[1, s],
            recv_sem=halo_recv.at[0, s],
            device_id=right,
            device_id_type=MESH,
        )

    def own_plane(s):
        base[...] = in_plane(xs[s].reshape(PLANES * 4, ROWS, LANES), weights).reshape(base.shape)

    def own_part(s, z):
        total = base[z]
        for k in range(1, 5):
            if z - k >= 0 and z + k < PLANES:
                total = total + COEF[k] * (xs[s, z - k] + xs[s, z + k])
            elif z - k >= 0:
                total = total + COEF[k] * xs[s, z - k]
            elif z + k < PLANES:
                total = total + COEF[k] * xs[s, z + k]
        return total

    def halo_part(s, z, scale):
        parts = [(scale * COEF[k]) * halo_lo[s, 4 + z - k] for k in range(1, 5) if z - k < 0]
        parts += [(scale * COEF[k]) * halo_hi[s, z + k - PLANES] for k in range(1, 5) if z + k >= PLANES]
        return sum(parts[1:], parts[0])

    def arrived(s, side):
        (to_right if side == 0 else to_left)(s).wait_recv()
        return range(4 * side, 4 * side + 4)

    def send(s, side):
        (to_left if side == 0 else to_right)(s).start()

    send(0, 0)
    send(0, 1)

    def stage(s, carry):
        last = s == 3
        weight = jnp.where((s == 0) | last, DT / 6.0, DT / 3.0).astype(jnp.float32)
        reach = jnp.where(s == 2, DT, 0.5 * DT).astype(jnp.float32)
        after = jnp.where(last, weight, reach)
        own_plane(s)
        for z in range(PLANES):
            k = slope(xs[s, z], own_part(s, z), pots[z, 0], pots[z, 1], pots[z, 2])
            for c in range(4):
                total = acc[z, c] + weight * k[c]
                acc[z, c] = total
                pre[z, c] = jnp.where(last, total, xs[0, z, c] + reach * k[c])
        for side in (0, 1):
            more = {}
            for z in arrived(s, side):
                more[z] = turned(halo_part(s, z, -0.5 * ALPHA))
                for c in range(4):
                    xs[s + 1, z, c] = pre[z, c] + after * more[z][c]
            send(s + 1, side)
            for z in more:
                for c in range(4):
                    acc[z, c] = acc[z, c] + weight * more[z][c]
        return carry

    lax.fori_loop(0, 4, stage, 0)

    own_plane(4)
    for z in range(PLANES):
        base[z] = own_part(4, z)
        x = xs[4, z]
        an_re = x[0] * x[2] + x[1] * x[3]
        an_im = x[1] * x[2] - x[0] * x[3]
        sums[0, z, 1] = jnp.where(top, an_re, pltpu.roll(an_im, 4, 0))
        sums[1, z, 1] = jnp.where(top, pltpu.roll(an_re, 4, 0), an_im)
    for side in (0, 1):
        for z in arrived(4, side):
            x = xs[4, z]
            lap = base[z] + halo_part(4, z, 1.0)
            base[z] = lap
            dense = x[2] * x[2] + x[3] * x[3]
            kinetic = x[2] * lap[2] + x[3] * lap[3]
            sums[0, z, 0] = jnp.where(top, dense, pltpu.roll(kinetic, 4, 0))
            sums[1, z, 0] = jnp.where(top, pltpu.roll(dense, 4, 0), kinetic)

    def copy_to(src, dst, send_sem, recv_sem, peer):
        copy = pltpu.make_async_remote_copy(
            src_ref=src,
            dst_ref=dst,
            send_sem=send_sem,
            recv_sem=recv_sem,
            device_id=peer,
            device_id_type=MESH,
        )
        copy.start()
        return copy

    order = sorted(range(1, n), key=lambda d: -min(d, n - d))
    first_copies = []
    for d in order + [0]:
        planes = pl.ds(second_at[d] * share, share)
        first_copies.append(
            copy_to(sums.at[1 - core, planes], piece_in.at[n + d], first_send.at[n + d], first_recv.at[n + d], second_cross[d])
        )
        if d > 0:
            planes = pl.ds(first_at[d] * share, share)
            first_copies.append(
                copy_to(sums.at[core, planes], piece_in.at[d], first_send.at[d], first_recv.at[d], first_peer[d])
            )
    total = sums[core, pl.ds(first * share, share)]
    for copy in first_copies:
        copy.wait_recv()
    for d in range(1, 2 * n):
        total = total + piece_in[d]
    gather_in[0] = total

    second_copies = [
        copy_to(gather_in.at[0], gather_in.at[d], second_send.at[d - 1], second_recv.at[d - 1], second_peer[d])
        for d in order
    ]
    for copy in second_copies:
        copy.wait_recv()
    total = gather_in[second]
    for i in range(1, n):
        total = total + gather_in[lax.rem(second + n - i, n)]

    for z in range(share):
        s01, s23 = total[z, 0], total[z, 1]
        density = (2.0 / modes_total) * s01
        kinetic = (-2.0 / modes_total) * pltpu.roll(s01, 4, 0)
        an_re = (1.0 / modes_total) * s23
        an_im = (1.0 / modes_total) * pltpu.roll(s23, 4, 0)
        dense = jnp.where(top, density, jnp.float32(1.0)) + EPS
        third_root = jnp.exp(jnp.log(dense) * (-1.0 / 3.0))
        fermi = (0.5 * (3.0 * math.pi**2) ** (2.0 / 3.0)) * (dense * third_root)
        an_sq = an_re * an_re + an_im * an_im
        f0 = BETA * fermi - (GAMMA / 3.0) * an_sq * third_root / dense
        f1 = -GAMMA * an_re * third_root
        f2 = -GAMMA * an_im * third_root
        f3 = (0.5 * ALPHA) * kinetic + (0.6 * BETA) * dense * fermi + GAMMA * an_sq * third_root
        field_mine[0, z, 0] = jnp.where(top, f0, pltpu.roll(f1, 4, 0))
        field_mine[0, z, 1] = jnp.where(top, f2, pltpu.roll(f3, 4, 0))

    back_copies = []
    for d in order + [0]:
        back_copies.append(
            copy_to(field_mine.at[0], field_other.at[d], back_send.at[n + d], back_recv.at[n + d], first_cross[d])
        )
        if d > 0:
            back_copies.append(copy_to(field_mine.at[0], field_mine.at[d], back_send.at[d], back_recv.at[d], first_peer[d]))
    for copy in back_copies:
        copy.wait_recv()

    even = core == 0
    for z in range(PLANES):
        place, part = z // share, z % share
        mine = field_mine[lax.rem(first + n - place, n), part]
        other = field_other[lax.rem(second + n - place, n), part]
        fields = []
        for p in range(2):
            low = jnp.where(even, mine[p], other[p])
            high = jnp.where(even, other[p], mine[p])
            fields.append(jnp.where(top, low, pltpu.roll(high, 4, 0)))
            fields.append(jnp.where(top, pltpu.roll(low, 4, 0), high))
        for c in range(3):
            pots[z, c] = fields[c]
        for c in range(4):
            field_rows[c, z * ROWS : (z + 1) * ROWS, :] = fields[c]
        x = xs[4, z]
        k = slope(x, base[z], fields[0], fields[1], fields[2])
        for c in range(4):
            acc[z, c] = x[c] + (DT / 6.0) * k[c]
            xs[5, z, c] = x[c] + (0.5 * DT) * k[c]
        if z == 3:
            send(5, 0)
    send(5, 1)
    own_plane(5)
    for z in range(PLANES):
        k = slope(xs[5, z], own_part(5, z), pots[z, 0], pots[z, 1], pots[z, 2])
        for c in range(4):
            acc[z, c] = acc[z, c] + (DT / 3.0) * k[c]
    for side in (0, 1):
        for z in arrived(5, side):
            more = turned(halo_part(5, z, -0.5 * ALPHA * DT / 3.0))
            for c in range(4):
                out_rows[c, z * ROWS : (z + 1) * ROWS, :] = acc[z, c] + more[c]

    for s in range(6):
        to_left(s).wait_send()
        to_right(s).wait_send()
    for copy in first_copies + second_copies + back_copies:
        copy.wait_send()


def unpack(out_rows, field_rows, uo_ref, vo_ref, fo_ref, outs, sems):
    copies = [
        pltpu.make_async_copy(outs.at[0:4], fo_ref, sems.at[0]),
        pltpu.make_async_copy(outs.at[4:6], uo_ref.at[0], sems.at[1]),
        pltpu.make_async_copy(outs.at[6:8], vo_ref.at[0], sems.at[2]),
    ]
    for c in range(8):
        source = field_rows if c < 4 else out_rows
        for t in range(ROWS):
            outs[c, :, t * LANES : (t + 1) * LANES] = source[c % 4, pl.ds(t, PLANES, stride=ROWS), :]
        if c in (3, 5, 7):
            copies[(c - 3) // 2].start()
    for copy in copies:
        copy.wait()


def solution(mesh):
    modes, grid_n = mesh.shape["modes"], mesh.shape["grid"]
    n = math.isqrt(modes // 2)
    share = PLANES // n
    f32 = jnp.float32
    plane = (ROWS, LANES)
    vmem = pl.BlockSpec(memory_space=pltpu.VMEM)
    hbm = pl.BlockSpec(memory_space=pltpu.HBM)

    def local(u_modes, v_modes, potential, pairing):
        out_rows, field_rows = pl.pallas_call(
            functools.partial(kernel, n, grid_n, float(modes)),
            out_shape=(jax.ShapeDtypeStruct((4, PLANES * ROWS, LANES), f32),) * 2,
            in_specs=[hbm] * 4,
            out_specs=(vmem, vmem),
            scratch_shapes=[
                pltpu.VMEM((7, PLANES, ROWS * LANES), f32),
                pltpu.VMEM((7, PLANES * ROWS, LANES), f32),
                pltpu.VMEM((6, PLANES, 4) + plane, f32),
                pltpu.VMEM((PLANES, 3) + plane, f32),
                pltpu.VMEM((PLANES, 4) + plane, f32),
                pltpu.VMEM((PLANES, 4) + plane, f32),
                pltpu.VMEM((PLANES, 4) + plane, f32),
                pltpu.VMEM((6, 4, 4) + plane, f32),
                pltpu.VMEM((6, 4, 4) + plane, f32),
                pltpu.VMEM((2, PLANES, 2) + plane, f32),
                pltpu.VMEM((2 * n, share, 2) + plane, f32),
                pltpu.VMEM((n, share, 2) + plane, f32),
                pltpu.VMEM((n, share, 2) + plane, f32),
                pltpu.VMEM((n, share, 2) + plane, f32),
                pltpu.VMEM((3, 2 * LANES, 2 * LANES), jnp.bfloat16),
                pltpu.SemaphoreType.DMA((4,)),
                pltpu.SemaphoreType.DMA((2, 6)),
                pltpu.SemaphoreType.DMA((2, 6)),
                pltpu.SemaphoreType.DMA((2 * n,)),
                pltpu.SemaphoreType.DMA((2 * n,)),
                pltpu.SemaphoreType.DMA((n - 1,)),
                pltpu.SemaphoreType.DMA((n - 1,)),
                pltpu.SemaphoreType.DMA((2 * n,)),
                pltpu.SemaphoreType.DMA((2 * n,)),
            ],
            compiler_params=pltpu.CompilerParams(
                collective_id=0, has_side_effects=True, vmem_limit_bytes=16 * 1024 * 1024
            ),
        )(*(pltpu.with_memory_space_constraint(x, pltpu.HBM) for x in (u_modes, v_modes, potential, pairing)))
        return pl.pallas_call(
            unpack,
            out_shape=(
                jax.ShapeDtypeStruct(u_modes.shape, f32),
                jax.ShapeDtypeStruct(v_modes.shape, f32),
                jax.ShapeDtypeStruct((4,) + potential.shape, f32),
            ),
            in_specs=[vmem, vmem],
            out_specs=(hbm, hbm, hbm),
            scratch_shapes=[
                pltpu.VMEM((8, PLANES, ROWS * LANES), f32),
                pltpu.SemaphoreType.DMA((3,)),
            ],
            compiler_params=pltpu.CompilerParams(vmem_limit_bytes=16 * 1024 * 1024),
        )(out_rows, field_rows)

    placed = (
        P("modes", None, "grid", None),
        P("modes", None, "grid", None),
        P("grid", None),
        P(None, "grid", None),
    )
    return jax.shard_map(
        local,
        mesh=mesh,
        in_specs=placed,
        out_specs=(placed[0], placed[1], placed[3]),
        check_vma=False,
    )
```

```python
import functools
import math

import jax
import jax.numpy as jnp
from jax import lax
from jax.experimental import pallas as pl
from jax.experimental.pallas import tpu as pltpu
from jax.sharding import PartitionSpec as P

MESH = pl.DeviceIdType.MESH
COEF = (-205.0 / 72.0, 8.0 / 5.0, -1.0 / 5.0, 8.0 / 315.0, -1.0 / 560.0)
ALPHA = 1.14
BETA = -0.553
GAMMA = -11.11
DT = 0.18
EPS = 1e-06
PLANES = 8
ROWS = 8
LANES = 128


def spread(weights):
    source = lax.broadcasted_iota(jnp.int32, (LANES, LANES), 0)
    target = lax.broadcasted_iota(jnp.int32, (LANES, LANES), 1)
    dx = lax.rem(lax.rem(source, 32) + 32 - lax.rem(target, 32), 32)
    dy = source // 32 - target // 32
    zero = jnp.zeros((LANES, LANES), jnp.float32)
    within, above, below = zero, zero, zero
    for k in range(1, 5):
        within = jnp.where((dy == 0) & ((dx == k) | (dx == 32 - k)), COEF[k], within)
        within = jnp.where((dx == 0) & ((dy == k) | (dy == -k)), COEF[k], within)
        above = jnp.where((dx == 0) & (dy + 4 == k), COEF[k], above)
        below = jnp.where((dx == 0) & (4 - dy == k), COEF[k], below)
    for i, part in enumerate((within, above, below)):
        high = part.astype(jnp.bfloat16)
        low = (part - high.astype(jnp.float32)).astype(jnp.bfloat16)
        for half in range(2):
            weights[i, LANES * half : LANES * (half + 1), 0:LANES] = high
            weights[i, LANES * half : LANES * (half + 1), LANES : 2 * LANES] = low


def in_plane(x, weights):
    flat = x.reshape(-1, LANES)
    high = flat.astype(jnp.bfloat16)
    low = (flat - high.astype(jnp.float32)).astype(jnp.bfloat16)
    both = jnp.concatenate([high, low], axis=1)

    def times(i):
        wide = jnp.dot(both, weights[i], preferred_element_type=jnp.float32)
        return (wide[:, :LANES] + wide[:, LANES:]).reshape(x.shape)

    return (3.0 * COEF[0]) * x + times(0) + pltpu.roll(times(1), ROWS - 1, 1) + pltpu.roll(times(2), 1, 1)


def slope(x, lap, pot, pr, pi):
    kin = [(-0.5 * ALPHA) * lap[c] + pot * x[c] for c in range(4)]
    return [
        kin[1] + pr * x[3] + pi * x[2],
        pi * x[3] - pr * x[2] - kin[0],
        pr * x[1] - pi * x[0] - kin[3],
        kin[2] - pr * x[0] - pi * x[1],
    ]


def kernel(
    n,
    grid_n,
    modes_total,
    u_ref,
    v_ref,
    pot_ref,
    pair_ref,
    out_rows,
    field_rows,
    raws,
    rows,
    wide,
    inner,
    middle,
    pots,
    acc,
    base,
    own,
    sums,
    taus,
    piece_in,
    gather_in,
    field_mine,
    field_other,
    tau_piece,
    tau_gather,
    energy_mine,
    energy_other,
    weights,
    load_sem,
    ring_send,
    ring_recv,
    first_send,
    first_recv,
    second_send,
    second_recv,
    back_send,
    back_recv,
):
    m = lax.axis_index("modes")
    g = lax.axis_index("grid")
    core = lax.rem(m, 2)
    yy = lax.rem(m // 2, n)
    zz = m // (2 * n)
    left = (m, lax.rem(g + grid_n - 1, grid_n))
    right = (m, lax.rem(g + 1, grid_n))
    flip = 1 - 2 * core
    first = yy + core * (zz - yy)
    second = zz + core * (yy - zz)
    first_base = (1 - core) * zz * 2 * n + core * (yy * 2 + 1)
    first_step = 2 + core * (2 * n - 2)
    second_base = (1 - core) * yy * 2 + core * (zz * 2 * n + 1)
    second_step = 2 * n - core * (2 * n - 2)
    share = PLANES // n
    first_at = [lax.rem(first + d, n) for d in range(n)]
    second_at = [lax.rem(second + d, n) for d in range(n)]
    first_peer = [(first_base + at * first_step, g) for at in first_at]
    second_peer = [(second_base + at * second_step, g) for at in second_at]
    first_cross = [(peer[0] + flip, g) for peer in first_peer]
    second_cross = [(peer[0] + flip, g) for peer in second_peer]
    order = sorted(range(1, n), key=lambda d: -min(d, n - d))
    started = []

    def remote(src, dst, send_sem, recv_sem, peer):
        copy = pltpu.make_async_remote_copy(
            src_ref=src,
            dst_ref=dst,
            send_sem=send_sem,
            recv_sem=recv_sem,
            device_id=peer,
            device_id_type=MESH,
        )
        started.append(copy)
        return copy

    def to_left(k, src, dst):
        return remote(src, dst, ring_send.at[0, k], ring_recv.at[0, k], left)

    def to_right(k, src, dst):
        return remote(src, dst, ring_send.at[1, k], ring_recv.at[1, k], right)

    barrier = pltpu.get_barrier_semaphore()
    partners = [left, right] + first_cross + first_peer[1:] + second_peer[1:] + second_cross[1:]
    for partner in partners:
        pl.semaphore_signal(barrier, inc=1, device_id=partner, device_id_type=MESH)

    loads = [
        pltpu.make_async_copy(u_ref.at[0], raws.at[1, 0:2], load_sem.at[0]),
        pltpu.make_async_copy(v_ref.at[0], raws.at[1, 2:4], load_sem.at[1]),
        pltpu.make_async_copy(pot_ref, raws.at[1, 4], load_sem.at[2]),
        pltpu.make_async_copy(pair_ref, raws.at[1, 5:7], load_sem.at[3]),
    ]
    for load in loads:
        load.start()
    low, high = slice(0, 4), slice(4, 8)
    start_copies = [[], []]
    for k, planes in ((0, (low, high)), (2, (high, low))):
        for side, send in enumerate((to_left, to_right)):
            place = 2 - 2 * side
            at = planes[side]
            start_copies[side] += [
                send(k, u_ref.at[0, :, at, :], raws.at[place, 0:2, at, :]),
                send(k + 1, v_ref.at[0, :, at, :], raws.at[place, 2:4, at, :]),
            ]
    for side, send in enumerate((to_left, to_right)):
        place = 2 - 2 * side
        at = (low, high)[side]
        start_copies[side] += [
            send(4, pot_ref.at[at, :], raws.at[place, 4, at, :]),
            send(5, pair_ref.at[:, at, :], raws.at[place, 5:7, at, :]),
        ]
    pl.semaphore_wait(barrier, len(partners))
    for i in (0, 1, 4, 5, 2, 3):
        for side in (0, 1):
            start_copies[side][i].start()

    spread(weights)
    row = lax.broadcasted_iota(jnp.int32, (ROWS, LANES), 0)
    top = row < 4

    def planes_of(place, comps, at):
        for c in comps:
            for t in range(ROWS):
                piece = raws[place, c, at, t * LANES : (t + 1) * LANES]
                rows[c, t * PLANES + at.start : t * PLANES + at.stop, :] = piece
        for c in comps:
            for z in range(at.start, at.stop):
                yield c, z, rows[c, pl.ds(z, ROWS, stride=PLANES), :]

    def flat_plane(x):
        return in_plane(x.reshape(-1, ROWS, LANES), weights).reshape(x.shape)

    def depth(ref, z):
        total = COEF[1] * (ref[z - 1] + ref[z + 1])
        for k in range(2, 5):
            total = total + COEF[k] * (ref[z - k] + ref[z + k])
        return total

    for load in loads:
        load.wait()
    for c, z, value in planes_of(1, range(7), slice(0, 8)):
        if c < 4:
            wide[0, 8 + z, c] = value
        else:
            pots[4 + z, c - 4] = value

    def section(s, arrive, reach, weight):
        def advance(z):
            lap = base[z - 4] + depth(wide.at[s], z)
            k = slope(wide[s, z], lap, pots[z - 4, 0], pots[z - 4, 1], pots[z - 4, 2])
            for c in range(4):
                inner[z - 4, c] = wide[0, z, c] + reach * k[c]
                if 8 <= z < 16:
                    acc[z - 8, c] = (wide[0, z, c] if s == 0 else acc[z - 8, c]) + weight * k[c]

        base[4:12] = flat_plane(wide[s, 8:16])
        for side in (0, 1):
            arrive(side, 0)
            for z in range(8 + 4 * side, 12 + 4 * side):
                advance(z)
        own[...] = flat_plane(inner[4:12])
        base[0:4] = flat_plane(wide[s, 4:8])
        base[12:16] = flat_plane(wide[s, 16:20])
        for side in (0, 1):
            arrive(side, 1)
            for z in range(4 + 12 * side, 8 + 12 * side):
                advance(z)

    def second_slope(z):
        lap = own[z] + depth(inner, z + 4)
        return slope(inner[z + 4], lap, pots[z + 4, 0], pots[z + 4, 1], pots[z + 4, 2])

    def arrive_start(side, far):
        copies = start_copies[1 - side]
        place, at = ((0, (high, low)), (2, (low, high)))[side]
        for copy in copies[2:4] if far else copies[0:2]:
            copy.wait_recv()
        for c, z, value in planes_of(place, range(4), at[far]):
            wide[0, 8 * place + z, c] = value
        if far:
            for copy in copies[4:6]:
                copy.wait_recv()
            for c, z, value in planes_of(place, range(4, 7), at[0]):
                pots[8 * place - 4 + z, c - 4] = value

    section(0, arrive_start, 0.5 * DT, DT / 6.0)
    near = [to_left(6, wide.at[1, 8:12], wide.at[1, 16:20]), to_right(6, wide.at[1, 12:16], wide.at[1, 4:8])]
    far = [to_left(7, wide.at[1, 12:16], wide.at[1, 20:24]), to_right(7, wide.at[1, 8:12], wide.at[1, 0:4])]
    for z in range(PLANES):
        k = second_slope(z)
        for c in range(4):
            wide[1, 8 + z, c] = wide[0, 8 + z, c] + (0.5 * DT) * k[c]
            acc[z, c] = acc[z, c] + (DT / 3.0) * k[c]
        if z == 3:
            near[0].start()
    near[1].start()
    far[0].start()
    far[1].start()

    def arrive_second(side, is_far):
        (far if is_far else near)[1 - side].wait_recv()

    section(1, arrive_second, DT, DT / 3.0)
    edge = [to_left(8, wide.at[2, 8:12], wide.at[2, 16:20]), to_right(8, wide.at[2, 12:16], wide.at[2, 4:8])]
    for z in range(PLANES):
        k = second_slope(z)
        x = [acc[z, c] + (DT / 6.0) * k[c] for c in range(4)]
        for c in range(4):
            wide[2, 8 + z, c] = x[c]
        dense = x[2] * x[2] + x[3] * x[3]
        an_re = x[0] * x[2] + x[1] * x[3]
        an_im = x[1] * x[2] - x[0] * x[3]
        sums[0, z, 0] = jnp.where(top, dense, pltpu.roll(an_re, 4, 0))
        sums[1, z, 0] = jnp.where(top, pltpu.roll(dense, 4, 0), an_re)
        sums[0, z, 1] = an_im
        sums[1, z, 1] = pltpu.roll(an_im, 4, 0)

    def to_owners(lot, src, piece):
        copies = []
        for d in order + [0]:
            planes = pl.ds(second_at[d] * share, share)
            at = (lot, n + d)
            copies.append(
                remote(src.at[1 - core, planes], piece.at[n + d], first_send.at[at], first_recv.at[at], second_cross[d])
            )
            if d > 0:
                planes = pl.ds(first_at[d] * share, share)
                copies.append(
                    remote(src.at[core, planes], piece.at[d], first_send.at[lot, d], first_recv.at[lot, d], first_peer[d])
                )
        for copy in copies:
            copy.start()
        return copies

    def summed(copies, src, piece):
        total = src[core, pl.ds(first * share, share)]
        for copy in copies:
            copy.wait_recv()
        for d in range(1, 2 * n):
            total = total + piece[d]
        return total

    def along_second(lot, gather, value):
        gather[0] = value
        copies = []
        for d in order:
            copy = remote(gather.at[0], gather.at[d], second_send.at[lot, d], second_recv.at[lot, d], second_peer[d])
            copy.start()
            copies.append(copy)
        return copies

    def gathered(copies, gather):
        for copy in copies:
            copy.wait_recv()
        total = gather[second]
        for i in range(1, n):
            total = total + gather[lax.rem(second + n - i, n)]
        return total

    def back(lot, mine, other):
        copies = []
        for d in order + [0]:
            at = (lot, n + d)
            copies.append(remote(mine.at[0], other.at[d], back_send.at[at], back_recv.at[at], first_cross[d]))
            if d > 0:
                copies.append(remote(mine.at[0], mine.at[d], back_send.at[lot, d], back_recv.at[lot, d], first_peer[d]))
        for copy in copies:
            copy.start()
        return copies

    main_first = to_owners(0, sums, piece_in)
    edge[0].start()
    edge[1].start()

    own[...] = flat_plane(wide[2, 8:16])
    for side in (0, 1):
        edge[1 - side].wait_recv()
        for z in range(4 * side, 4 * side + 4):
            lap = own[z]
            for k in range(1, 5):
                lap = lap + COEF[k] * (wide[2, 8 + z - k] + wide[2, 8 + z + k])
            own[z] = lap
            kinetic = wide[2, 8 + z, 2] * lap[2] + wide[2, 8 + z, 3] * lap[3]
            taus[0, z] = kinetic
            taus[1, z] = pltpu.roll(kinetic, 4, 0)
    tau_first = to_owners(1, taus, tau_piece)
    main_second = along_second(0, gather_in, summed(main_first, sums, piece_in))
    tau_second = along_second(1, tau_gather, summed(tau_first, taus, tau_piece))
    total = gathered(main_second, gather_in)

    rests = []
    for z in range(share):
        dense = jnp.where(top, (2.0 / modes_total) * total[z, 0], jnp.float32(1.0)) + EPS
        an_re = (1.0 / modes_total) * pltpu.roll(total[z, 0], 4, 0)
        an_im = (1.0 / modes_total) * total[z, 1]
        third_root = jnp.exp(jnp.log(dense) * (-1.0 / 3.0))
        fermi = (0.5 * (3.0 * math.pi**2) ** (2.0 / 3.0)) * (dense * third_root)
        an_sq = an_re * an_re + an_im * an_im
        f0 = BETA * fermi - (GAMMA / 3.0) * an_sq * third_root / dense
        f1 = -GAMMA * an_re * third_root
        f2 = -GAMMA * an_im * third_root
        rests.append((0.6 * BETA) * dense * fermi + GAMMA * an_sq * third_root)
        field_mine[0, z, 0] = jnp.where(top, f0, pltpu.roll(f1, 4, 0))
        field_mine[0, z, 1] = f2
    main_back = back(0, field_mine, field_other)
    tau_total = gathered(tau_second, tau_gather)
    for z in range(share):
        energy_mine[0, z] = (-ALPHA / modes_total) * tau_total[z] + rests[z]
    tau_back = back(1, energy_mine, energy_other)
    for copy in main_back:
        copy.wait_recv()

    even = core == 0
    swap = [to_left(9, middle.at[4:8], middle.at[12:16]), to_right(9, middle.at[8:12], middle.at[0:4])]

    def places(z):
        place = z // share
        return lax.rem(first + n - place, n), lax.rem(second + n - place, n), z % share

    for z in range(PLANES):
        at_mine, at_other, part = places(z)
        mine, other = field_mine[at_mine, part], field_other[at_other, part]
        lower = [jnp.where(even, mine[p], other[p]) for p in range(2)]
        upper = [jnp.where(even, other[p], mine[p]) for p in range(2)]
        fields = [
            jnp.where(top, lower[0], pltpu.roll(upper[0], 4, 0)),
            jnp.where(top, pltpu.roll(lower[0], 4, 0), upper[0]),
            jnp.where(top, lower[1], pltpu.roll(upper[1], 4, 0)),
        ]
        k = slope(wide[2, 8 + z], own[z], *fields)
        for c in range(3):
            pots[z + 4, c] = fields[c]
            field_rows[c, z * ROWS : (z + 1) * ROWS, :] = fields[c]
        for c in range(4):
            acc[z, c] = wide[2, 8 + z, c] + (DT / 6.0) * k[c]
            middle[4 + z, c] = wide[2, 8 + z, c] + (0.5 * DT) * k[c]
        if z == 3:
            swap[0].start()
    swap[1].start()
    own[...] = flat_plane(middle[4:12])
    for copy in tau_back:
        copy.wait_recv()
    for z in range(PLANES):
        at_mine, at_other, part = places(z)
        mine, other = energy_mine[at_mine, part], energy_other[at_other, part]
        lower, upper = jnp.where(even, mine, other), jnp.where(even, other, mine)
        field_rows[3, z * ROWS : (z + 1) * ROWS, :] = jnp.where(top, lower, pltpu.roll(upper, 4, 0))
    for side in (0, 1):
        swap[1 - side].wait_recv()
        for z in range(4 * side, 4 * side + 4):
            lap = own[z] + depth(middle, z + 4)
            k = slope(middle[4 + z], lap, pots[z + 4, 0], pots[z + 4, 1], pots[z + 4, 2])
            for c in range(4):
                out_rows[c, z * ROWS : (z + 1) * ROWS, :] = acc[z, c] + (DT / 3.0) * k[c]

    for copy in started:
        copy.wait_send()


def unpack(out_rows, field_rows, uo_ref, vo_ref, fo_ref, outs, sems):
    copies = [
        pltpu.make_async_copy(outs.at[0:4], fo_ref, sems.at[0]),
        pltpu.make_async_copy(outs.at[4:6], uo_ref.at[0], sems.at[1]),
        pltpu.make_async_copy(outs.at[6:8], vo_ref.at[0], sems.at[2]),
    ]
    for c in range(8):
        source = field_rows if c < 4 else out_rows
        for t in range(ROWS):
            outs[c, :, t * LANES : (t + 1) * LANES] = source[c % 4, pl.ds(t, PLANES, stride=ROWS), :]
        if c in (3, 5, 7):
            copies[(c - 3) // 2].start()
    for copy in copies:
        copy.wait()


def solution(mesh):
    modes, grid_n = mesh.shape["modes"], mesh.shape["grid"]
    n = math.isqrt(modes // 2)
    share = PLANES // n
    f32 = jnp.float32
    plane = (ROWS, LANES)
    vmem = pl.BlockSpec(memory_space=pltpu.VMEM)
    hbm = pl.BlockSpec(memory_space=pltpu.HBM)

    def local(u_modes, v_modes, potential, pairing):
        out_rows, field_rows = pl.pallas_call(
            functools.partial(kernel, n, grid_n, float(modes)),
            out_shape=(jax.ShapeDtypeStruct((4, PLANES * ROWS, LANES), f32),) * 2,
            in_specs=[hbm] * 4,
            out_specs=(vmem, vmem),
            scratch_shapes=[
                pltpu.VMEM((3, 7, PLANES, ROWS * LANES), f32),
                pltpu.VMEM((7, PLANES * ROWS, LANES), f32),
                pltpu.VMEM((3, 3 * PLANES, 4) + plane, f32),
                pltpu.VMEM((2 * PLANES, 4) + plane, f32),
                pltpu.VMEM((2 * PLANES, 4) + plane, f32),
                pltpu.VMEM((2 * PLANES, 3) + plane, f32),
                pltpu.VMEM((PLANES, 4) + plane, f32),
                pltpu.VMEM((2 * PLANES, 4) + plane, f32),
                pltpu.VMEM((PLANES, 4) + plane, f32),
                pltpu.VMEM((2, PLANES, 2) + plane, f32),
                pltpu.VMEM((2, PLANES) + plane, f32),
                pltpu.VMEM((2 * n, share, 2) + plane, f32),
                pltpu.VMEM((n, share, 2) + plane, f32),
                pltpu.VMEM((n, share, 2) + plane, f32),
                pltpu.VMEM((n, share, 2) + plane, f32),
                pltpu.VMEM((2 * n, share) + plane, f32),
                pltpu.VMEM((n, share) + plane, f32),
                pltpu.VMEM((n, share) + plane, f32),
                pltpu.VMEM((n, share) + plane, f32),
                pltpu.VMEM((3, 2 * LANES, 2 * LANES), jnp.bfloat16),
                pltpu.SemaphoreType.DMA((4,)),
                pltpu.SemaphoreType.DMA((2, 10)),
                pltpu.SemaphoreType.DMA((2, 10)),
                pltpu.SemaphoreType.DMA((2, 2 * n)),
                pltpu.SemaphoreType.DMA((2, 2 * n)),
                pltpu.SemaphoreType.DMA((2, n)),
                pltpu.SemaphoreType.DMA((2, n)),
                pltpu.SemaphoreType.DMA((2, 2 * n)),
                pltpu.SemaphoreType.DMA((2, 2 * n)),
            ],
            compiler_params=pltpu.CompilerParams(
                collective_id=0, has_side_effects=True, vmem_limit_bytes=16 * 1024 * 1024
            ),
        )(*(pltpu.with_memory_space_constraint(x, pltpu.HBM) for x in (u_modes, v_modes, potential, pairing)))
        return pl.pallas_call(
            unpack,
            out_shape=(
                jax.ShapeDtypeStruct(u_modes.shape, f32),
                jax.ShapeDtypeStruct(v_modes.shape, f32),
                jax.ShapeDtypeStruct((4,) + potential.shape, f32),
            ),
            in_specs=[vmem, vmem],
            out_specs=(hbm, hbm, hbm),
            scratch_shapes=[
                pltpu.VMEM((8, PLANES, ROWS * LANES), f32),
                pltpu.SemaphoreType.DMA((3,)),
            ],
            compiler_params=pltpu.CompilerParams(vmem_limit_bytes=16 * 1024 * 1024),
        )(out_rows, field_rows)

    placed = (
        P("modes", None, "grid", None),
        P("modes", None, "grid", None),
        P("grid", None),
        P(None, "grid", None),
    )
    return jax.shard_map(
        local,
        mesh=mesh,
        in_specs=placed,
        out_specs=(placed[0], placed[1], placed[3]),
        check_vma=False,
    )
```

```python
import functools
import math

import jax
import jax.numpy as jnp
from jax import lax
from jax.experimental import pallas as pl
from jax.experimental.pallas import tpu as pltpu
from jax.sharding import PartitionSpec as P

MESH = pl.DeviceIdType.MESH
COEF = (-205.0 / 72.0, 8.0 / 5.0, -1.0 / 5.0, 8.0 / 315.0, -1.0 / 560.0)
ALPHA = 1.14
BETA = -0.553
GAMMA = -11.11
DT = 0.18
EPS = 1e-06
PLANES = 8
ROWS = 8
LANES = 128


def spread(weights):
    source = lax.broadcasted_iota(jnp.int32, (LANES, LANES), 0)
    target = lax.broadcasted_iota(jnp.int32, (LANES, LANES), 1)
    dx = lax.rem(lax.rem(source, 32) + 32 - lax.rem(target, 32), 32)
    dy = source // 32 - target // 32
    zero = jnp.zeros((LANES, LANES), jnp.float32)
    within, above, below = zero, zero, zero
    for k in range(1, 5):
        within = jnp.where((dy == 0) & ((dx == k) | (dx == 32 - k)), COEF[k], within)
        within = jnp.where((dx == 0) & ((dy == k) | (dy == -k)), COEF[k], within)
        above = jnp.where((dx == 0) & (dy + 4 == k), COEF[k], above)
        below = jnp.where((dx == 0) & (4 - dy == k), COEF[k], below)
    for i, part in enumerate((within, above, below)):
        high = part.astype(jnp.bfloat16)
        low = (part - high.astype(jnp.float32)).astype(jnp.bfloat16)
        for half in range(2):
            weights[i, LANES * half : LANES * (half + 1), 0:LANES] = high
            weights[i, LANES * half : LANES * (half + 1), LANES : 2 * LANES] = low


def in_plane(x, weights):
    flat = x.reshape(-1, LANES)
    high = flat.astype(jnp.bfloat16)
    low = (flat - high.astype(jnp.float32)).astype(jnp.bfloat16)
    both = jnp.concatenate([high, low], axis=1)

    def times(i):
        wide = jnp.dot(both, weights[i], preferred_element_type=jnp.float32)
        return (wide[:, :LANES] + wide[:, LANES:]).reshape(x.shape)

    return (3.0 * COEF[0]) * x + times(0) + pltpu.roll(times(1), ROWS - 1, 1) + pltpu.roll(times(2), 1, 1)


def slope(x, lap, pot, pr, pi):
    kin = [(-0.5 * ALPHA) * lap[c] + pot * x[c] for c in range(4)]
    return [
        kin[1] + pr * x[3] + pi * x[2],
        pi * x[3] - pr * x[2] - kin[0],
        pr * x[1] - pi * x[0] - kin[3],
        kin[2] - pr * x[0] - pi * x[1],
    ]


def kernel(
    n,
    grid_n,
    modes_total,
    u_ref,
    v_ref,
    pot_ref,
    pair_ref,
    out_rows,
    field_rows,
    raw,
    rows,
    wide,
    inner,
    middle,
    pots,
    acc,
    base,
    own,
    sums,
    taus,
    piece_in,
    gather_in,
    field_mine,
    field_other,
    tau_piece,
    tau_gather,
    energy_mine,
    energy_other,
    weights,
    load_sem,
    ring_send,
    ring_recv,
    y_send,
    y_recv,
    z_send,
    z_recv,
    back_send,
    back_recv,
):
    m = lax.axis_index("modes")
    g = lax.axis_index("grid")
    core = lax.rem(m, 2)
    yy = lax.rem(m // 2, n)
    zz = m // (2 * n)
    left = (m, lax.rem(g + grid_n - 1, grid_n))
    right = (m, lax.rem(g + 1, grid_n))
    flip = 1 - 2 * core
    share = PLANES // n
    y_at = [lax.rem(yy + d, n) for d in range(n)]
    y_peer = [(zz * 2 * n + at * 2 + core, g) for at in y_at]
    y_cross = [(peer[0] + flip, g) for peer in y_peer]
    z_peer = [(lax.rem(zz + d, n) * 2 * n + yy * 2 + core, g) for d in range(n)]
    order = sorted(range(1, n), key=lambda d: -min(d, n - d))
    order_z = sorted(range(1, n), key=lambda d: min(d, n - d))
    started = []

    def remote(src, dst, send_sem, recv_sem, peer):
        copy = pltpu.make_async_remote_copy(
            src_ref=src,
            dst_ref=dst,
            send_sem=send_sem,
            recv_sem=recv_sem,
            device_id=peer,
            device_id_type=MESH,
        )
        started.append(copy)
        return copy

    def to_left(k, src, dst):
        return remote(src, dst, ring_send.at[0, k], ring_recv.at[0, k], left)

    def to_right(k, src, dst):
        return remote(src, dst, ring_send.at[1, k], ring_recv.at[1, k], right)

    barrier = pltpu.get_barrier_semaphore()
    partners = [left, right] + y_cross + y_peer[1:] + z_peer[1:]
    for partner in partners[0:2]:
        pl.semaphore_signal(barrier, inc=1, device_id=partner, device_id_type=MESH)

    loads = [
        pltpu.make_async_copy(u_ref.at[0], raw.at[0:2], load_sem.at[0]),
        pltpu.make_async_copy(v_ref.at[0], raw.at[2:4], load_sem.at[1]),
        pltpu.make_async_copy(pot_ref, raw.at[4], load_sem.at[2]),
        pltpu.make_async_copy(pair_ref, raw.at[5:7], load_sem.at[3]),
    ]
    for load in loads:
        load.start()
    for partner in partners[2:]:
        pl.semaphore_signal(barrier, inc=1, device_id=partner, device_id_type=MESH)
    row = lax.broadcasted_iota(jnp.int32, (ROWS, LANES), 0)
    top = row < 4

    def flat_plane(x):
        return in_plane(x.reshape(-1, ROWS, LANES), weights).reshape(x.shape)

    def depth(ref, z):
        total = COEF[1] * (ref[z - 1] + ref[z + 1])
        for k in range(2, 5):
            total = total + COEF[k] * (ref[z - k] + ref[z + k])
        return total

    for load in loads:
        load.wait()
    for c in range(7):
        for t in range(ROWS):
            rows[c, t * PLANES : (t + 1) * PLANES, :] = raw[c, :, t * LANES : (t + 1) * LANES]
    for c in range(7):
        for z in range(PLANES):
            value = rows[c, pl.ds(z, ROWS, stride=PLANES), :]
            if c < 4:
                wide[0, 8 + z, c] = value
            else:
                pots[4 + z, c - 4] = value

    def near_far(s, k):
        state = wide.at[s]
        near = [to_left(k, state.at[8:12], state.at[16:20]), to_right(k, state.at[12:16], state.at[4:8])]
        far = [to_left(k + 1, state.at[12:16], state.at[20:24]), to_right(k + 1, state.at[8:12], state.at[0:4])]
        return near, far

    start_near, start_far = near_far(0, 0)
    start_pots = [to_left(2, pots.at[4:8], pots.at[12:16]), to_right(2, pots.at[8:12], pots.at[0:4])]
    pl.semaphore_wait(barrier, len(partners))
    for copy in start_near + start_far + start_pots:
        copy.start()
    spread(weights)

    def section(s, arrive, reach, weight):
        def advance(z):
            lap = base[z - 4] + depth(wide.at[s], z)
            k = slope(wide[s, z], lap, pots[z - 4, 0], pots[z - 4, 1], pots[z - 4, 2])
            for c in range(4):
                inner[z - 4, c] = wide[0, z, c] + reach * k[c]
                if 8 <= z < 16:
                    acc[z - 8, c] = (wide[0, z, c] if s == 0 else acc[z - 8, c]) + weight * k[c]

        base[4:12] = flat_plane(wide[s, 8:16])
        for side in (0, 1):
            arrive(side, 0)
            for z in range(8 + 4 * side, 12 + 4 * side):
                advance(z)
        own[...] = flat_plane(inner[4:12])
        base[0:4] = flat_plane(wide[s, 4:8])
        base[12:16] = flat_plane(wide[s, 16:20])
        for side in (0, 1):
            arrive(side, 1)
            for z in range(4 + 12 * side, 8 + 12 * side):
                advance(z)

    def second_slope(z):
        lap = own[z] + depth(inner, z + 4)
        return slope(inner[z + 4], lap, pots[z + 4, 0], pots[z + 4, 1], pots[z + 4, 2])

    def arrive_start(side, is_far):
        (start_far if is_far else start_near)[1 - side].wait_recv()
        if is_far:
            start_pots[1 - side].wait_recv()

    section(0, arrive_start, 0.5 * DT, DT / 6.0)
    near, far = near_far(1, 3)
    for z in range(PLANES):
        k = second_slope(z)
        for c in range(4):
            wide[1, 8 + z, c] = wide[0, 8 + z, c] + (0.5 * DT) * k[c]
            acc[z, c] = acc[z, c] + (DT / 3.0) * k[c]
        if z == 3:
            near[0].start()
    near[1].start()
    far[0].start()
    far[1].start()

    def arrive_second(side, is_far):
        (far if is_far else near)[1 - side].wait_recv()

    section(1, arrive_second, DT, DT / 3.0)
    state = wide.at[2]
    edges = []
    for k, c in ((5, slice(2, 4)), (6, slice(0, 2))):
        edges.append(to_left(k, state.at[8:12, c], state.at[16:20, c]))
        edges.append(to_right(k, state.at[12:16, c], state.at[4:8, c]))
    for z in range(PLANES):
        k = second_slope(z)
        x = [acc[z, c] + (DT / 6.0) * k[c] for c in range(4)]
        for c in range(4):
            wide[2, 8 + z, c] = x[c]
        dense = x[2] * x[2] + x[3] * x[3]
        an_re = x[0] * x[2] + x[1] * x[3]
        an_im = x[1] * x[2] - x[0] * x[3]
        sums[0, z, 0:8] = jnp.where(top, dense, pltpu.roll(an_re, 4, 0))
        sums[1, z, 0:8] = jnp.where(top, pltpu.roll(dense, 4, 0), an_re)
        sums[0, z, 8:12] = an_im[0:4]
        sums[1, z, 8:12] = pltpu.roll(an_im, 4, 0)[0:4]

    def to_owners(lot, src, piece):
        copies = []
        for d in order + [0]:
            planes = pl.ds(y_at[d] * share, share)
            for cross, peer in ((1, y_cross[d]), (0, y_peer[d])):
                if cross or d > 0:
                    half, at = (1 - core, n + d) if cross else (core, d)
                    copies.append(
                        remote(src.at[half, planes], piece.at[at], y_send.at[lot, at], y_recv.at[lot, at], peer)
                    )
        for copy in copies:
            copy.start()
        return copies

    def summed(copies, src, piece):
        total = src[core, pl.ds(yy * share, share)]
        for copy in copies:
            copy.wait_recv()
        for d in range(1, 2 * n):
            total = total + piece[d]
        return total

    def along_z(lot, gather, value):
        gather[0] = value
        copies = []
        for d in order_z:
            copy = remote(gather.at[0], gather.at[d], z_send.at[lot, d], z_recv.at[lot, d], z_peer[d])
            copy.start()
            copies.append(copy)
        return copies

    def gathered(copies, gather):
        for copy in copies:
            copy.wait_recv()
        total = gather[zz]
        for i in range(1, n):
            total = total + gather[lax.rem(zz + n - i, n)]
        return total

    def back(lot, mine, other):
        copies = []
        for d in order + [0]:
            copies.append(remote(mine.at[0], other.at[d], back_send.at[lot, n + d], back_recv.at[lot, n + d], y_cross[d]))
            if d > 0:
                copies.append(remote(mine.at[0], mine.at[d], back_send.at[lot, d], back_recv.at[lot, d], y_peer[d]))
        for copy in copies:
            copy.start()
        return copies

    main_first = to_owners(0, sums, piece_in)
    for copy in edges:
        copy.start()

    own[...] = flat_plane(wide[2, 8:16])
    for comps, copies in ((slice(2, 4), edges[0:2]), (slice(0, 2), edges[2:4])):
        for side in (0, 1):
            copies[1 - side].wait_recv()
            for z in range(4 * side, 4 * side + 4):
                lap = own[z, comps]
                for k in range(1, 5):
                    lap = lap + COEF[k] * (wide[2, 8 + z - k, comps] + wide[2, 8 + z + k, comps])
                own[z, comps] = lap
                if comps.start == 2:
                    kinetic = wide[2, 8 + z, 2] * lap[0] + wide[2, 8 + z, 3] * lap[1]
                    taus[0, z] = kinetic[0:4]
                    taus[1, z] = pltpu.roll(kinetic, 4, 0)[0:4]
        if comps.start == 2:
            tau_first = to_owners(1, taus, tau_piece)
    main_second = along_z(0, gather_in, summed(main_first, sums, piece_in))
    tau_second = along_z(1, tau_gather, summed(tau_first, taus, tau_piece))
    total = gathered(main_second, gather_in)

    rests = []
    for z in range(share):
        dense = (2.0 / modes_total) * total[z, 0:4] + EPS
        an_re = (1.0 / modes_total) * pltpu.roll(total[z, 0:8], 4, 0)[0:4]
        an_im = (1.0 / modes_total) * total[z, 8:12]
        third_root = jnp.exp(jnp.log(dense) * (-1.0 / 3.0))
        fermi = (0.5 * (3.0 * math.pi**2) ** (2.0 / 3.0)) * (dense * third_root)
        an_sq = an_re * an_re + an_im * an_im
        f0 = BETA * fermi - (GAMMA / 3.0) * an_sq * third_root / dense
        f1 = -GAMMA * an_re * third_root
        f2 = -GAMMA * an_im * third_root
        rests.append((0.6 * BETA) * dense * fermi + GAMMA * an_sq * third_root)
        field_mine[0, z, 0:4] = f0
        field_mine[0, z, 4:8] = f1
        field_mine[0, z, 8:12] = f2
    earlier = list(started)
    main_back = back(0, field_mine, field_other)
    tau_total = gathered(tau_second, tau_gather)
    for z in range(share):
        energy_mine[0, z] = (-ALPHA / modes_total) * tau_total[z] + rests[z]
    tau_back = back(1, energy_mine, energy_other)
    for copy in earlier:
        copy.wait_send()
    for copy in main_back:
        copy.wait_recv()

    even = core == 0
    swap = [to_left(7, middle.at[4:8], middle.at[12:16]), to_right(7, middle.at[8:12], middle.at[0:4])]

    def places(z):
        place = z // share
        return lax.rem(yy + n - place, n), z % share

    for z in range(PLANES):
        at, part = places(z)
        mine, other = field_mine[at, part], field_other[at, part]
        lower, upper = jnp.where(even, mine, other), jnp.where(even, other, mine)
        fields = [
            jnp.where(top, lower[0:8], pltpu.roll(upper[0:8], 4, 0)),
            jnp.where(top, pltpu.roll(lower[0:8], 4, 0), upper[0:8]),
            jnp.concatenate([lower[8:12], upper[8:12]], axis=0),
        ]
        k = slope(wide[2, 8 + z], own[z], *fields)
        for c in range(3):
            pots[z + 4, c] = fields[c]
            field_rows[c, z * ROWS : (z + 1) * ROWS, :] = fields[c]
        for c in range(4):
            acc[z, c] = wide[2, 8 + z, c] + (DT / 6.0) * k[c]
            middle[4 + z, c] = wide[2, 8 + z, c] + (0.5 * DT) * k[c]
        if z == 3:
            swap[0].start()
    swap[1].start()
    own[...] = flat_plane(middle[4:12])
    for copy in tau_back:
        copy.wait_recv()
    for copy in main_back + tau_back:
        copy.wait_send()
    for z in range(PLANES):
        at, part = places(z)
        mine, other = energy_mine[at, part], energy_other[at, part]
        lower, upper = jnp.where(even, mine, other), jnp.where(even, other, mine)
        field_rows[3, z * ROWS : (z + 1) * ROWS, :] = jnp.concatenate([lower, upper], axis=0)
    for side in (0, 1):
        swap[1 - side].wait_recv()
        for z in range(4 * side, 4 * side + 4):
            lap = own[z] + depth(middle, z + 4)
            k = slope(middle[4 + z], lap, pots[z + 4, 0], pots[z + 4, 1], pots[z + 4, 2])
            for c in range(4):
                out_rows[c, z * ROWS : (z + 1) * ROWS, :] = acc[z, c] + (DT / 3.0) * k[c]

    for copy in swap:
        copy.wait_send()


def unpack(out_rows, field_rows, uo_ref, vo_ref, fo_ref, outs, sems):
    copies = [
        pltpu.make_async_copy(outs.at[0:4], fo_ref, sems.at[0]),
        pltpu.make_async_copy(outs.at[4:6], uo_ref.at[0], sems.at[1]),
        pltpu.make_async_copy(outs.at[6:8], vo_ref.at[0], sems.at[2]),
    ]
    for c in range(8):
        source = field_rows if c < 4 else out_rows
        for t in range(ROWS):
            outs[c, :, t * LANES : (t + 1) * LANES] = source[c % 4, pl.ds(t, PLANES, stride=ROWS), :]
        if c in (3, 5, 7):
            copies[(c - 3) // 2].start()
    for copy in copies:
        copy.wait()


def solution(mesh):
    modes, grid_n = mesh.shape["modes"], mesh.shape["grid"]
    n = math.isqrt(modes // 2)
    share = PLANES // n
    f32 = jnp.float32
    plane = (ROWS, LANES)
    vmem = pl.BlockSpec(memory_space=pltpu.VMEM)
    hbm = pl.BlockSpec(memory_space=pltpu.HBM)

    def local(u_modes, v_modes, potential, pairing):
        out_rows, field_rows = pl.pallas_call(
            functools.partial(kernel, n, grid_n, float(modes)),
            out_shape=(jax.ShapeDtypeStruct((4, PLANES * ROWS, LANES), f32),) * 2,
            in_specs=[hbm] * 4,
            out_specs=(vmem, vmem),
            scratch_shapes=[
                pltpu.VMEM((7, PLANES, ROWS * LANES), f32),
                pltpu.VMEM((7, PLANES * ROWS, LANES), f32),
                pltpu.VMEM((3, 3 * PLANES, 4) + plane, f32),
                pltpu.VMEM((2 * PLANES, 4) + plane, f32),
                pltpu.VMEM((2 * PLANES, 4) + plane, f32),
                pltpu.VMEM((2 * PLANES, 3) + plane, f32),
                pltpu.VMEM((PLANES, 4) + plane, f32),
                pltpu.VMEM((2 * PLANES, 4) + plane, f32),
                pltpu.VMEM((PLANES, 4) + plane, f32),
                pltpu.VMEM((2, PLANES, 12, LANES), f32),
                pltpu.VMEM((2, PLANES, 4, LANES), f32),
                pltpu.VMEM((2 * n, share, 12, LANES), f32),
                pltpu.VMEM((n, share, 12, LANES), f32),
                pltpu.VMEM((n, share, 12, LANES), f32),
                pltpu.VMEM((n, share, 12, LANES), f32),
                pltpu.VMEM((2 * n, share, 4, LANES), f32),
                pltpu.VMEM((n, share, 4, LANES), f32),
                pltpu.VMEM((n, share, 4, LANES), f32),
                pltpu.VMEM((n, share, 4, LANES), f32),
                pltpu.VMEM((3, 2 * LANES, 2 * LANES), jnp.bfloat16),
                pltpu.SemaphoreType.DMA((4,)),
                pltpu.SemaphoreType.DMA((2, 8)),
                pltpu.SemaphoreType.DMA((2, 8)),
                pltpu.SemaphoreType.DMA((2, 2 * n)),
                pltpu.SemaphoreType.DMA((2, 2 * n)),
                pltpu.SemaphoreType.DMA((2, n)),
                pltpu.SemaphoreType.DMA((2, n)),
                pltpu.SemaphoreType.DMA((2, 2 * n)),
                pltpu.SemaphoreType.DMA((2, 2 * n)),
            ],
            compiler_params=pltpu.CompilerParams(
                collective_id=0, has_side_effects=True, vmem_limit_bytes=16 * 1024 * 1024
            ),
        )(*(pltpu.with_memory_space_constraint(x, pltpu.HBM) for x in (u_modes, v_modes, potential, pairing)))
        return pl.pallas_call(
            unpack,
            out_shape=(
                jax.ShapeDtypeStruct(u_modes.shape, f32),
                jax.ShapeDtypeStruct(v_modes.shape, f32),
                jax.ShapeDtypeStruct((4,) + potential.shape, f32),
            ),
            in_specs=[vmem, vmem],
            out_specs=(hbm, hbm, hbm),
            scratch_shapes=[
                pltpu.VMEM((8, PLANES, ROWS * LANES), f32),
                pltpu.SemaphoreType.DMA((3,)),
            ],
            compiler_params=pltpu.CompilerParams(vmem_limit_bytes=16 * 1024 * 1024),
        )(out_rows, field_rows)

    placed = (
        P("modes", None, "grid", None),
        P("modes", None, "grid", None),
        P("grid", None),
        P(None, "grid", None),
    )
    return jax.shard_map(
        local,
        mesh=mesh,
        in_specs=placed,
        out_specs=(placed[0], placed[1], placed[3]),
        check_vma=False,
    )
```

```python
import functools
import math

import jax
import jax.numpy as jnp
from jax import lax
from jax.experimental import pallas as pl
from jax.experimental.pallas import tpu as pltpu
from jax.sharding import PartitionSpec as P

MESH = pl.DeviceIdType.MESH
COEF = (-205.0 / 72.0, 8.0 / 5.0, -1.0 / 5.0, 8.0 / 315.0, -1.0 / 560.0)
ALPHA = 1.14
BETA = -0.553
GAMMA = -11.11
DT = 0.18
EPS = 1e-06
PLANES = 8
ROWS = 8
LANES = 128


def spread(weights):
    source = lax.broadcasted_iota(jnp.int32, (LANES, LANES), 0)
    target = lax.broadcasted_iota(jnp.int32, (LANES, LANES), 1)
    dx = lax.rem(lax.rem(source, 32) + 32 - lax.rem(target, 32), 32)
    dy = source // 32 - target // 32
    zero = jnp.zeros((LANES, LANES), jnp.float32)
    within, above, below = zero, zero, zero
    for k in range(1, 5):
        within = jnp.where((dy == 0) & ((dx == k) | (dx == 32 - k)), COEF[k], within)
        within = jnp.where((dx == 0) & ((dy == k) | (dy == -k)), COEF[k], within)
        above = jnp.where((dx == 0) & (dy + 4 == k), COEF[k], above)
        below = jnp.where((dx == 0) & (4 - dy == k), COEF[k], below)
    for i, part in enumerate((within, above, below)):
        high = part.astype(jnp.bfloat16)
        low = (part - high.astype(jnp.float32)).astype(jnp.bfloat16)
        for half in range(2):
            weights[i, LANES * half : LANES * (half + 1), 0:LANES] = high
            weights[i, LANES * half : LANES * (half + 1), LANES : 2 * LANES] = low


def in_plane(x, weights):
    flat = x.reshape(-1, LANES)
    high = flat.astype(jnp.bfloat16)
    low = (flat - high.astype(jnp.float32)).astype(jnp.bfloat16)
    both = jnp.concatenate([high, low], axis=1)

    def times(i):
        wide = jnp.dot(both, weights[i], preferred_element_type=jnp.float32)
        return (wide[:, :LANES] + wide[:, LANES:]).reshape(x.shape)

    return (3.0 * COEF[0]) * x + times(0) + pltpu.roll(times(1), ROWS - 1, 1) + pltpu.roll(times(2), 1, 1)


def slope(x, lap, pot, pr, pi):
    kin = [(-0.5 * ALPHA) * lap[c] + pot * x[c] for c in range(4)]
    return [
        kin[1] + pr * x[3] + pi * x[2],
        pi * x[3] - pr * x[2] - kin[0],
        pr * x[1] - pi * x[0] - kin[3],
        kin[2] - pr * x[0] - pi * x[1],
    ]


def kernel(
    n,
    grid_n,
    modes_total,
    u_ref,
    v_ref,
    pot_ref,
    pair_ref,
    out_rows,
    field_rows,
    raw,
    rows,
    wide,
    inner,
    middle,
    pots,
    acc,
    base,
    own,
    sums,
    taus,
    piece_in,
    gather_in,
    field_mine,
    field_other,
    tau_piece,
    tau_gather,
    energy_mine,
    energy_other,
    weights,
    load_sem,
    ring_send,
    ring_recv,
    y_send,
    y_recv,
    z_send,
    z_recv,
    back_send,
    back_recv,
):
    m = lax.axis_index("modes")
    g = lax.axis_index("grid")
    core = lax.rem(m, 2)
    yy = lax.rem(m // 2, n)
    zz = m // (2 * n)
    left = (m, lax.rem(g + grid_n - 1, grid_n))
    right = (m, lax.rem(g + 1, grid_n))
    flip = 1 - 2 * core
    share = PLANES // n
    y_at = [lax.rem(yy + d, n) for d in range(n)]
    y_peer = [(zz * 2 * n + at * 2 + core, g) for at in y_at]
    y_cross = [(peer[0] + flip, g) for peer in y_peer]
    z_peer = [(lax.rem(zz + d, n) * 2 * n + yy * 2 + core, g) for d in range(n)]
    order = sorted(range(1, n), key=lambda d: -min(d, n - d))
    order_z = sorted(range(1, n), key=lambda d: min(d, n - d))
    started = []

    def remote(src, dst, send_sem, recv_sem, peer):
        copy = pltpu.make_async_remote_copy(
            src_ref=src,
            dst_ref=dst,
            send_sem=send_sem,
            recv_sem=recv_sem,
            device_id=peer,
            device_id_type=MESH,
        )
        started.append(copy)
        return copy

    def to_left(k, src, dst):
        return remote(src, dst, ring_send.at[0, k], ring_recv.at[0, k], left)

    def to_right(k, src, dst):
        return remote(src, dst, ring_send.at[1, k], ring_recv.at[1, k], right)

    barrier = pltpu.get_barrier_semaphore()
    partners = [left, right] + y_cross + y_peer[1:] + z_peer[1:]
    for partner in partners[0:2]:
        pl.semaphore_signal(barrier, inc=1, device_id=partner, device_id_type=MESH)

    loads = [
        pltpu.make_async_copy(u_ref.at[0], raw.at[0:2], load_sem.at[0]),
        pltpu.make_async_copy(v_ref.at[0], raw.at[2:4], load_sem.at[1]),
        pltpu.make_async_copy(pot_ref, raw.at[4], load_sem.at[2]),
        pltpu.make_async_copy(pair_ref, raw.at[5:7], load_sem.at[3]),
    ]
    for load in loads:
        load.start()
    for partner in partners[2:]:
        pl.semaphore_signal(barrier, inc=1, device_id=partner, device_id_type=MESH)
    row = lax.broadcasted_iota(jnp.int32, (ROWS, LANES), 0)
    top = row < 4

    def flat_plane(x):
        return in_plane(x.reshape(-1, ROWS, LANES), weights).reshape(x.shape)

    def depth(ref, z):
        total = COEF[1] * (ref[z - 1] + ref[z + 1])
        for k in range(2, 5):
            total = total + COEF[k] * (ref[z - k] + ref[z + k])
        return total

    for load in loads:
        load.wait()
    for c in range(7):
        for t in range(ROWS):
            rows[c, t * PLANES : (t + 1) * PLANES, :] = raw[c, :, t * LANES : (t + 1) * LANES]
    for c in range(7):
        for z in range(PLANES):
            value = rows[c, pl.ds(z, ROWS, stride=PLANES), :]
            if c < 4:
                wide[0, 8 + z, c] = value
            else:
                pots[4 + z, c - 4] = value

    def near_far(s, k):
        state = wide.at[s]
        near = [to_left(k, state.at[8:12], state.at[16:20]), to_right(k, state.at[12:16], state.at[4:8])]
        far = [to_left(k + 1, state.at[12:16], state.at[20:24]), to_right(k + 1, state.at[8:12], state.at[0:4])]
        return near, far

    start_near, start_far = near_far(0, 0)
    start_pots = [to_left(2, pots.at[4:8], pots.at[12:16]), to_right(2, pots.at[8:12], pots.at[0:4])]
    pl.semaphore_wait(barrier, len(partners))
    for copy in start_near + start_far + start_pots:
        copy.start()
    spread(weights)

    def section(s, arrive, reach, weight):
        def advance(z):
            lap = base[z - 4] + depth(wide.at[s], z)
            k = slope(wide[s, z], lap, pots[z - 4, 0], pots[z - 4, 1], pots[z - 4, 2])
            for c in range(4):
                inner[z - 4, c] = wide[0, z, c] + reach * k[c]
                if 8 <= z < 16:
                    acc[z - 8, c] = (wide[0, z, c] if s == 0 else acc[z - 8, c]) + weight * k[c]

        base[4:12] = flat_plane(wide[s, 8:16])
        for side in (0, 1):
            arrive(side, 0)
            for z in range(8 + 4 * side, 12 + 4 * side):
                advance(z)
        own[...] = flat_plane(inner[4:12])
        base[0:4] = flat_plane(wide[s, 4:8])
        base[12:16] = flat_plane(wide[s, 16:20])
        for side in (0, 1):
            arrive(side, 1)
            for z in range(4 + 12 * side, 8 + 12 * side):
                advance(z)

    def second_slope(z):
        lap = own[z] + depth(inner, z + 4)
        return slope(inner[z + 4], lap, pots[z + 4, 0], pots[z + 4, 1], pots[z + 4, 2])

    def arrive_start(side, is_far):
        (start_far if is_far else start_near)[1 - side].wait_recv()
        if is_far:
            start_pots[1 - side].wait_recv()

    section(0, arrive_start, 0.5 * DT, DT / 6.0)
    near, far = near_far(1, 3)
    for z in range(PLANES):
        k = second_slope(z)
        for c in range(4):
            wide[1, 8 + z, c] = wide[0, 8 + z, c] + (0.5 * DT) * k[c]
            acc[z, c] = acc[z, c] + (DT / 3.0) * k[c]
        if z == 3:
            near[0].start()
    near[1].start()
    far[0].start()
    far[1].start()

    def arrive_second(side, is_far):
        (far if is_far else near)[1 - side].wait_recv()

    section(1, arrive_second, DT, DT / 3.0)
    state = wide.at[2]
    edges = []
    for k, c in ((5, slice(2, 4)), (6, slice(0, 2))):
        edges.append(to_left(k, state.at[8:12, c], state.at[16:20, c]))
        edges.append(to_right(k, state.at[12:16, c], state.at[4:8, c]))
    for z in range(PLANES):
        k = second_slope(z)
        x = [acc[z, c] + (DT / 6.0) * k[c] for c in range(4)]
        for c in range(4):
            wide[2, 8 + z, c] = x[c]
        dense = x[2] * x[2] + x[3] * x[3]
        an_re = x[0] * x[2] + x[1] * x[3]
        an_im = x[1] * x[2] - x[0] * x[3]
        sums[0, z, 0:8] = jnp.where(top, dense, pltpu.roll(an_re, 4, 0))
        sums[1, z, 0:8] = jnp.where(top, pltpu.roll(dense, 4, 0), an_re)
        sums[0, z, 8:12] = an_im[0:4]
        sums[1, z, 8:12] = pltpu.roll(an_im, 4, 0)[0:4]

    def to_owners(lot, src, piece):
        copies = []
        for d in order + [0]:
            planes = pl.ds(y_at[d] * share, share)
            for cross, peer in ((1, y_cross[d]), (0, y_peer[d])):
                if cross or d > 0:
                    half, at = (1 - core, n + d) if cross else (core, d)
                    copies.append(
                        remote(src.at[half, planes], piece.at[at], y_send.at[lot, at], y_recv.at[lot, at], peer)
                    )
        for copy in copies:
            copy.start()
        return copies

    def summed(copies, src, piece):
        total = src[core, pl.ds(yy * share, share)]
        for copy in copies:
            copy.wait_recv()
        for d in range(1, 2 * n):
            total = total + piece[d]
        return total

    def along_z(lot, gather, value):
        gather[0] = value
        copies = []
        for d in order_z:
            copy = remote(gather.at[0], gather.at[d], z_send.at[lot, d], z_recv.at[lot, d], z_peer[d])
            copy.start()
            copies.append(copy)
        return copies

    def gathered(copies, gather):
        for copy in copies:
            copy.wait_recv()
        total = gather[zz]
        for i in range(1, n):
            total = total + gather[lax.rem(zz + n - i, n)]
        return total

    def back(lot, mine, other):
        copies = []
        for d in order + [0]:
            copies.append(remote(mine.at[0], other.at[d], back_send.at[lot, n + d], back_recv.at[lot, n + d], y_cross[d]))
            if d > 0:
                copies.append(remote(mine.at[0], mine.at[d], back_send.at[lot, d], back_recv.at[lot, d], y_peer[d]))
        for copy in copies:
            copy.start()
        return copies

    main_first = to_owners(0, sums, piece_in)
    for copy in edges:
        copy.start()

    own[...] = flat_plane(wide[2, 8:16])
    for comps, copies in ((slice(2, 4), edges[0:2]), (slice(0, 2), edges[2:4])):
        for side in (0, 1):
            copies[1 - side].wait_recv()
            for z in range(4 * side, 4 * side + 4):
                lap = own[z, comps]
                for k in range(1, 5):
                    lap = lap + COEF[k] * (wide[2, 8 + z - k, comps] + wide[2, 8 + z + k, comps])
                own[z, comps] = lap
                if comps.start == 2:
                    kinetic = wide[2, 8 + z, 2] * lap[0] + wide[2, 8 + z, 3] * lap[1]
                    taus[0, z] = kinetic[0:4]
                    taus[1, z] = pltpu.roll(kinetic, 4, 0)[0:4]
        if comps.start == 2:
            tau_first = to_owners(1, taus, tau_piece)
    main_second = along_z(0, gather_in, summed(main_first, sums, piece_in))
    tau_second = along_z(1, tau_gather, summed(tau_first, taus, tau_piece))
    total = gathered(main_second, gather_in)

    rests = []
    for z in range(share):
        dense = (2.0 / modes_total) * total[z, 0:4] + EPS
        an_re = (1.0 / modes_total) * pltpu.roll(total[z, 0:8], 4, 0)[0:4]
        an_im = (1.0 / modes_total) * total[z, 8:12]
        third_root = jnp.exp(jnp.log(dense) * (-1.0 / 3.0))
        fermi = (0.5 * (3.0 * math.pi**2) ** (2.0 / 3.0)) * (dense * third_root)
        an_sq = an_re * an_re + an_im * an_im
        f0 = BETA * fermi - (GAMMA / 3.0) * an_sq * third_root / dense
        f1 = -GAMMA * an_re * third_root
        f2 = -GAMMA * an_im * third_root
        rests.append((0.6 * BETA) * dense * fermi + GAMMA * an_sq * third_root)
        field_mine[0, z, 0:4] = f0
        field_mine[0, z, 4:8] = f1
        field_mine[0, z, 8:12] = f2
    earlier = list(started)
    main_back = back(0, field_mine, field_other)
    tau_total = gathered(tau_second, tau_gather)
    for z in range(share):
        energy_mine[0, z] = (-ALPHA / modes_total) * tau_total[z] + rests[z]
    tau_back = back(1, energy_mine, energy_other)
    for copy in earlier:
        copy.wait_send()
    for copy in main_back:
        copy.wait_recv()

    even = core == 0
    swap = [to_left(7, middle.at[4:8], middle.at[12:16]), to_right(7, middle.at[8:12], middle.at[0:4])]

    def places(z):
        place = z // share
        return lax.rem(yy + n - place, n), z % share

    for z in range(PLANES):
        at, part = places(z)
        mine, other = field_mine[at, part], field_other[at, part]
        lower, upper = jnp.where(even, mine, other), jnp.where(even, other, mine)
        fields = [
            jnp.where(top, lower[0:8], pltpu.roll(upper[0:8], 4, 0)),
            jnp.where(top, pltpu.roll(lower[0:8], 4, 0), upper[0:8]),
            jnp.concatenate([lower[8:12], upper[8:12]], axis=0),
        ]
        k = slope(wide[2, 8 + z], own[z], *fields)
        for c in range(3):
            pots[z + 4, c] = fields[c]
            field_rows[c, z * ROWS : (z + 1) * ROWS, :] = fields[c]
        for c in range(4):
            acc[z, c] = wide[2, 8 + z, c] + (DT / 6.0) * k[c]
            middle[4 + z, c] = wide[2, 8 + z, c] + (0.5 * DT) * k[c]
        if z == 3:
            swap[0].start()
    swap[1].start()
    own[...] = flat_plane(middle[4:12])
    for copy in tau_back:
        copy.wait_recv()
    for copy in main_back + tau_back:
        copy.wait_send()
    for z in range(PLANES):
        at, part = places(z)
        mine, other = energy_mine[at, part], energy_other[at, part]
        lower, upper = jnp.where(even, mine, other), jnp.where(even, other, mine)
        field_rows[3, z * ROWS : (z + 1) * ROWS, :] = jnp.concatenate([lower, upper], axis=0)
    for z in range(PLANES):
        lap = own[z]
        for k in range(1, 5):
            if z - k >= 0:
                lap = lap + COEF[k] * middle[z + 4 - k]
            if z + k < PLANES:
                lap = lap + COEF[k] * middle[z + 4 + k]
        k = slope(middle[4 + z], lap, pots[z + 4, 0], pots[z + 4, 1], pots[z + 4, 2])
        for c in range(4):
            acc[z, c] = acc[z, c] + (DT / 3.0) * k[c]
    scale = -0.5 * ALPHA * DT / 3.0
    for side in (0, 1):
        swap[1 - side].wait_recv()
        for z in range(4 * side, 4 * side + 4):
            parts = [(scale * COEF[k]) * middle[z + 4 - k] for k in range(1, 5) if z - k < 0]
            parts += [(scale * COEF[k]) * middle[z + 4 + k] for k in range(1, 5) if z + k >= PLANES]
            h = sum(parts[1:], parts[0])
            more = [h[1], -h[0], -h[3], h[2]]
            for c in range(4):
                out_rows[c, z * ROWS : (z + 1) * ROWS, :] = acc[z, c] + more[c]

    for copy in swap:
        copy.wait_send()


def unpack(out_rows, field_rows, uo_ref, vo_ref, fo_ref, outs, sems):
    copies = [
        pltpu.make_async_copy(outs.at[0:4], fo_ref, sems.at[0]),
        pltpu.make_async_copy(outs.at[4:6], uo_ref.at[0], sems.at[1]),
        pltpu.make_async_copy(outs.at[6:8], vo_ref.at[0], sems.at[2]),
    ]
    for c in range(8):
        source = field_rows if c < 4 else out_rows
        for t in range(ROWS):
            outs[c, :, t * LANES : (t + 1) * LANES] = source[c % 4, pl.ds(t, PLANES, stride=ROWS), :]
        if c in (3, 5, 7):
            copies[(c - 3) // 2].start()
    for copy in copies:
        copy.wait()


def solution(mesh):
    modes, grid_n = mesh.shape["modes"], mesh.shape["grid"]
    n = math.isqrt(modes // 2)
    share = PLANES // n
    f32 = jnp.float32
    plane = (ROWS, LANES)
    vmem = pl.BlockSpec(memory_space=pltpu.VMEM)
    hbm = pl.BlockSpec(memory_space=pltpu.HBM)

    def local(u_modes, v_modes, potential, pairing):
        out_rows, field_rows = pl.pallas_call(
            functools.partial(kernel, n, grid_n, float(modes)),
            out_shape=(jax.ShapeDtypeStruct((4, PLANES * ROWS, LANES), f32),) * 2,
            in_specs=[hbm] * 4,
            out_specs=(vmem, vmem),
            scratch_shapes=[
                pltpu.VMEM((7, PLANES, ROWS * LANES), f32),
                pltpu.VMEM((7, PLANES * ROWS, LANES), f32),
                pltpu.VMEM((3, 3 * PLANES, 4) + plane, f32),
                pltpu.VMEM((2 * PLANES, 4) + plane, f32),
                pltpu.VMEM((2 * PLANES, 4) + plane, f32),
                pltpu.VMEM((2 * PLANES, 3) + plane, f32),
                pltpu.VMEM((PLANES, 4) + plane, f32),
                pltpu.VMEM((2 * PLANES, 4) + plane, f32),
                pltpu.VMEM((PLANES, 4) + plane, f32),
                pltpu.VMEM((2, PLANES, 12, LANES), f32),
                pltpu.VMEM((2, PLANES, 4, LANES), f32),
                pltpu.VMEM((2 * n, share, 12, LANES), f32),
                pltpu.VMEM((n, share, 12, LANES), f32),
                pltpu.VMEM((n, share, 12, LANES), f32),
                pltpu.VMEM((n, share, 12, LANES), f32),
                pltpu.VMEM((2 * n, share, 4, LANES), f32),
                pltpu.VMEM((n, share, 4, LANES), f32),
                pltpu.VMEM((n, share, 4, LANES), f32),
                pltpu.VMEM((n, share, 4, LANES), f32),
                pltpu.VMEM((3, 2 * LANES, 2 * LANES), jnp.bfloat16),
                pltpu.SemaphoreType.DMA((4,)),
                pltpu.SemaphoreType.DMA((2, 8)),
                pltpu.SemaphoreType.DMA((2, 8)),
                pltpu.SemaphoreType.DMA((2, 2 * n)),
                pltpu.SemaphoreType.DMA((2, 2 * n)),
                pltpu.SemaphoreType.DMA((2, n)),
                pltpu.SemaphoreType.DMA((2, n)),
                pltpu.SemaphoreType.DMA((2, 2 * n)),
                pltpu.SemaphoreType.DMA((2, 2 * n)),
            ],
            compiler_params=pltpu.CompilerParams(
                collective_id=0, has_side_effects=True, vmem_limit_bytes=16 * 1024 * 1024
            ),
        )(*(pltpu.with_memory_space_constraint(x, pltpu.HBM) for x in (u_modes, v_modes, potential, pairing)))
        return pl.pallas_call(
            unpack,
            out_shape=(
                jax.ShapeDtypeStruct(u_modes.shape, f32),
                jax.ShapeDtypeStruct(v_modes.shape, f32),
                jax.ShapeDtypeStruct((4,) + potential.shape, f32),
            ),
            in_specs=[vmem, vmem],
            out_specs=(hbm, hbm, hbm),
            scratch_shapes=[
                pltpu.VMEM((8, PLANES, ROWS * LANES), f32),
                pltpu.SemaphoreType.DMA((3,)),
            ],
            compiler_params=pltpu.CompilerParams(vmem_limit_bytes=16 * 1024 * 1024),
        )(out_rows, field_rows)

    placed = (
        P("modes", None, "grid", None),
        P("modes", None, "grid", None),
        P("grid", None),
        P(None, "grid", None),
    )
    return jax.shard_map(
        local,
        mesh=mesh,
        in_specs=placed,
        out_specs=(placed[0], placed[1], placed[3]),
        check_vma=False,
    )
```
